128 devices in a mesh: seq: 32 (over z, x, core), head: 4 (over y).
Axes of the slice: x: 4, y: 4, z: 4, core: 2. Of those that a mesh axis runs over, the one named last changes fastest.
Arguments:
- keys_cache: bfloat16 [32, 16384, 1024], P(None, 'seq', 'head'), may hold values from -6 to 6
- values_cache: bfloat16 [32, 16384, 1024], P(None, 'seq', 'head'), may hold values from -6 to 6
- keep_blocks: int32 [32, 8, 128], P(None, 'head'), may hold values from 0 to 255, as said below
- keep_count: int32 [32, 8], P(None, 'head'), may hold values from 0 to 128, as said below
- queries: bfloat16 [3, 32, 8192], P(None, 'seq', 'head'), may hold values from -104 to 104
- new_keys: bfloat16 [3, 32, 1024], P(None, 'seq', 'head'), may hold values from -4.5 to 4.5
- new_values: bfloat16 [3, 32, 1024], P(None, 'seq', 'head'), may hold values from -6 to 6
- residual_in: bfloat16 [3, 32, 8192], P(None, None, 'seq'), may hold values from -40 to 40
- norm_gain: bfloat16 [8192], P('seq'), may hold values from 0.099609375 to 1.8984375
- w_out: bfloat16 [8192, 8192], P('head', 'seq'), may hold values from -0.375 to 0.375
- w_gate: bfloat16 [8192, 16384], P('seq', 'head'), may hold values from -0.0625 to 0.0625
- w_up: bfloat16 [8192, 16384], P('seq', 'head'), may hold values from -0.0625 to 0.0625
- w_down: bfloat16 [16384, 8192], P(('head', 'seq')), may hold values from -0.1875 to 0.1875
Outputs:
- attended: bfloat16 [3, 32, 8192], P(None, 'seq', 'head')
- layer_out: bfloat16 [3, 32, 8192], P(None, None, 'seq')
The draws below stay inside these ranges and needn't reach their ends.
Inputs may be any that keep to these rules, and one draw needn't show every extreme that they name: `keep_blocks`: entries below keep_count are distinct block numbers in increasing order, the rest are 0. Of one prompt and key-value head, at most 4 kept blocks lie in each aligned run of 8 blocks, and some run holds exactly 4. `keep_count`: some prompt and head keep 128 blocks.
All inputs are finite; a program needn't handle non-finite values.
Results may differ from the reference program's by a relative error of at most 0.009.
Values may be sent and summed in bfloat16 or wider, within the bound.
No kernel may reach another device: no remote copies, remote signals or barrier semaphores. Data moves between devices by JAX's collectives and lax.ppermute only.
A program may use at most 128 MiB of HBM per device.

```python
import math
import jax
import jax.numpy as jnp
from jax import lax

D = 8192
H = 64
KVH = 8
HD = 128
FF = 16384
BLK = 64
CAP = 4
STEPS = 3
S_DEV = 512
SEQ = 16384
B = 32
MAXK = 128


def block_plan(key):
    holders = MAXK // CAP
    per_dev = S_DEV // BLK
    first_key, second_key, third_key = jax.random.split(key, 3)
    counts = jax.random.randint(first_key, (B, KVH, holders), 0, CAP + 1)
    chosen = jax.random.randint(second_key, (), 0, B * KVH)
    pair_index = jnp.arange(B)[:, None] * KVH + jnp.arange(KVH)[None, :]
    counts = jnp.where((pair_index == chosen)[:, :, None], CAP, counts)
    scores = jax.random.randint(third_key, (B, KVH, holders, per_dev), 0, 1048576) * per_dev + jnp.arange(per_dev)
    block_rank = jnp.argsort(jnp.argsort(scores, axis=-1), axis=-1)
    kept_mask = (block_rank < counts[..., None]).reshape(B, KVH, holders * per_dev)
    block_index = jnp.arange(holders * per_dev)
    ordered = jnp.argsort(jnp.where(kept_mask, block_index, holders * per_dev + block_index), axis=-1)[..., :MAXK]
    kept_total = jnp.sum(counts, axis=-1)
    blocks = jnp.where(jnp.arange(MAXK) < kept_total[..., None], ordered, 0)
    return (blocks.astype(jnp.int32), kept_total.astype(jnp.int32))


def key_path(key):
    noise_draw = jnp.clip(jax.random.normal(key, (STEPS, B, KVH * HD)), -4.0, 4.0)
    path_rows = [noise_draw[0]]
    for step in range(1, STEPS):
        path_rows.append(noise_draw[step])
    return jnp.stack(path_rows)


def draw_keep_blocks(key, part):
    blocks, kept_total = block_plan(key)
    return blocks


def draw_keep_count(key, part):
    blocks, kept_total = block_plan(key)
    return kept_total


def draw_new_keys(key, part):
    return key_path(key).astype(jnp.bfloat16)


def draw_queries(key, part):
    key = jax.random.fold_in(key, 5)
    first_key = jax.random.fold_in(key, 0)
    return jnp.clip(1.5 * jax.random.normal(first_key, (STEPS, B, H * HD)), -9.0, 9.0).astype(jnp.bfloat16)


def draw_residual_in(key, part):
    key = jax.random.fold_in(key, 7)
    first_key = jax.random.fold_in(key, 0)
    column_rise = jnp.exp(math.log(3.0) * jnp.arange(D) / (D - 1))
    return jnp.clip(0.5 * jax.random.normal(first_key, (STEPS, B, D)) * column_rise, -20.0, 20.0).astype(jnp.bfloat16)


def strengthened(array, key, source, target, shards_of, factor):
    def block_of(axis_at):
        return (jnp.arange(array.shape[axis_at]) // (array.shape[axis_at] // shards_of)).reshape((-1,) + (1,) * (array.ndim - 1 - axis_at))

    first = jax.random.permutation(key, shards_of)[block_of(target)]
    far = (block_of(target) + shards_of // 2) % shards_of
    return jnp.where((block_of(source) == first) | (block_of(source) == far), factor * array, array)


def shard_levels(own_key, shape, pieces, low, high):
    factor_of, own = 1.0, jax.random.fold_in(own_key, 6)
    for axis_at, shards_of in pieces:
        heights = jnp.exp(jax.random.uniform(jax.random.fold_in(own, axis_at), (shards_of,), jnp.float32, low / len(pieces), high / len(pieces)))
        factor_of = factor_of * jnp.repeat(heights, shape[axis_at] // shards_of).reshape([-1 if axis == axis_at else 1 for axis in range(len(shape))])
    return factor_of


def scatter_about(key, extent, width, bound, cuts=(), kind=jnp.bfloat16):
    level = shard_levels(key, extent, cuts, -0.22, 0.18) if cuts else 1.0
    result = jax.random.normal(key, extent, jnp.float32) * width * level
    return jnp.minimum(jnp.maximum(result, -bound), bound).astype(kind)


def heavy_noise(rng, shape, spread, most, pieces, heavy, kind=jnp.bfloat16):
    array = spread * jax.random.normal(rng, shape, jnp.float32)
    if pieces:
        array = array * shard_levels(rng, shape, pieces, -0.22, 0.18)
    return jnp.clip(strengthened(array, jax.random.fold_in(rng, 3), *heavy), -most, most).astype(kind)


def setup_inputs(seed: int = 0) -> dict:
    keys = jax.random.split(jax.random.key(seed), 14)
    keys_cache = scatter_about(keys[0], (B, SEQ, KVH * HD), 1.0, 6.0, ((1, 32), (2, 4)))
    values_cache = scatter_about(keys[1], (B, SEQ, KVH * HD), 1.0, 6.0, ((1, 32), (2, 4)))
    keep_blocks = draw_keep_blocks(jax.random.fold_in(keys[13], 71), 0)
    keep_count = draw_keep_count(jax.random.fold_in(keys[13], 71), 0)
    queries = draw_queries(jax.random.fold_in(keys[13], 71), 0)
    new_keys = draw_new_keys(jax.random.fold_in(keys[13], 71), 0)
    new_values = scatter_about(keys[6], (STEPS, B, KVH * HD), 1.0, 6.0, ((1, 32), (2, 4)))
    residual_in = draw_residual_in(jax.random.fold_in(keys[13], 71), 0)
    norm_gain = jnp.clip(1.0 + 0.18 * jax.random.normal(keys[8], (D,), jnp.float32), 0.099609375, 1.8984375).astype(jnp.bfloat16)
    w_out = scatter_about(keys[9], (H * HD, D), (H * HD // 32) ** -0.5, 0.375, ((0, 4), (1, 32)))
    w_gate = scatter_about(keys[10], (D, FF), D ** -0.5, 0.0625, ((0, 32), (1, 4)))
    w_up = scatter_about(keys[11], (D, FF), D ** -0.5, 0.0625, ((0, 32), (1, 4)))
    w_down = heavy_noise(keys[12], (FF, D), FF ** -0.5, 0.1875, ((0, 128),), (0, 1, 128, 5.5))
    return {"keys_cache": keys_cache, "values_cache": values_cache, "keep_blocks": keep_blocks, "keep_count": keep_count, "queries": queries, "new_keys": new_keys, "new_values": new_values, "residual_in": residual_in, "norm_gain": norm_gain, "w_out": w_out, "w_gate": w_gate, "w_up": w_up, "w_down": w_down}


masked_score = -1e+30
norm_eps = 1e-06

def one_prompt(items):
    key_rows, value_rows, lists, kept_total, query_rows, nkey_rows, nvalue_rows = items
    groups = H // KVH
    key_table = key_rows.reshape(SEQ // BLK, BLK, KVH, HD).transpose(2, 0, 1, 3)
    value_table = value_rows.reshape(SEQ // BLK, BLK, KVH, HD).transpose(2, 0, 1, 3)
    picked_keys = jax.vmap(lambda table, lst: table[lst])(key_table, lists)
    picked_values = jax.vmap(lambda table, lst: table[lst])(value_table, lists)
    is_valid = jnp.arange(MAXK)[None, :] < kept_total[:, None]
    query_heads = query_rows.reshape(STEPS, KVH, groups, HD).astype(jnp.float32)
    score_scale = HD ** (-0.5)
    scores = jnp.einsum('thgd,hesd->thges', query_heads, picked_keys.astype(jnp.float32)) * score_scale
    scores = jnp.where(is_valid[None, :, None, :, None], scores, masked_score)
    new_heads = nkey_rows.reshape(STEPS, KVH, HD).astype(jnp.float32)
    new_scores = jnp.einsum('thgd,uhd->thgu', query_heads, new_heads) * score_scale
    causal = jnp.arange(STEPS)[:, None] >= jnp.arange(STEPS)[None, :]
    new_scores = jnp.where(causal[:, None, None, :], new_scores, masked_score)
    row_max = jnp.maximum(lax.optimization_barrier(jnp.max(scores, axis=(3, 4))), lax.optimization_barrier(jnp.max(new_scores, axis=3)))
    weight = jnp.exp(scores - row_max[..., None, None]).astype(jnp.bfloat16)
    new_weight = jnp.exp(new_scores - row_max[..., None]).astype(jnp.bfloat16)
    weight_sum = lax.optimization_barrier(jnp.sum(weight.astype(jnp.float32), axis=(3, 4))) + lax.optimization_barrier(jnp.sum(new_weight.astype(jnp.float32), axis=3))
    summed = jnp.einsum('thges,hesd->thgd', weight.astype(jnp.float32), picked_values.astype(jnp.float32))
    summed = summed + jnp.einsum('thgu,uhd->thgd', new_weight.astype(jnp.float32), nvalue_rows.reshape(STEPS, KVH, HD).astype(jnp.float32))
    return (summed / weight_sum[..., None]).astype(jnp.bfloat16).reshape(STEPS, H * HD)

def reference(keys_cache, values_cache, keep_blocks, keep_count, queries, new_keys, new_values, residual_in, norm_gain, w_out, w_gate, w_up, w_down):
    per_prompt = lax.map(one_prompt, (keys_cache, values_cache, keep_blocks, keep_count, queries.transpose(1, 0, 2), new_keys.transpose(1, 0, 2), new_values.transpose(1, 0, 2)))
    attended = per_prompt.transpose(1, 0, 2)
    token_count = STEPS * B
    projected = jnp.dot(attended.reshape(token_count, H * HD), w_out, preferred_element_type=jnp.float32)
    stream = residual_in.reshape(token_count, D).astype(jnp.float32) + projected
    mean_square = lax.optimization_barrier(jnp.mean(stream * stream, axis=1, keepdims=True))
    normed = (stream * lax.rsqrt(mean_square + norm_eps) * norm_gain.astype(jnp.float32)).astype(jnp.bfloat16)
    gate = jnp.dot(normed, w_gate, preferred_element_type=jnp.float32)
    up_part = jnp.dot(normed, w_up, preferred_element_type=jnp.float32)
    activated = (jax.nn.silu(gate) * up_part).astype(jnp.bfloat16)
    lowered = jnp.dot(activated, w_down, preferred_element_type=jnp.float32)
    layer_out = (stream + lowered).astype(jnp.bfloat16).reshape(STEPS, B, D)
    return (attended, layer_out)
```

```python
import functools

import jax
import jax.numpy as jnp
from jax import lax
from jax.experimental import pallas as pl
from jax.experimental.pallas import tpu as pltpu
from jax.sharding import PartitionSpec as P

D = 8192
H = 64
KVH = 8
HD = 128
BLK = 64
GROUPS = H // KVH

masked_score = -1e30
norm_eps = 1e-06
score_scale = HD ** (-0.5)

f32 = jnp.float32
bf16 = jnp.bfloat16

STEPS = 3
KV = 2
HQ = KV * GROUPS
ROWS = STEPS * HQ
PACK = ROWS + 16


def dot(a, b, ca=1, cb=0):
    return lax.dot_general(a, b, (((ca,), (cb,)), ((), ())), preferred_element_type=f32)


def first_head_rows():
    rows = lax.broadcasted_iota(jnp.int32, (ROWS, 1), 0)
    return (rows // GROUPS) % KV == 0


def two_head_queries(q, first):
    zero = jnp.zeros_like(q)
    return jnp.concatenate([jnp.where(first, q, zero), jnp.where(first, zero, q)], axis=1)


def per_head(values, first):
    return jnp.where(first, values[:, :HD], values[:, HD:])


def attend_kernel(per_dev, where_ref, lists_ref, q_own_ref, q_sib_ref, k_ref, v_ref, out_ref):
    base = where_ref[0] * per_dev
    core = where_ref[1]
    prompts = k_ref.shape[0]
    positions = k_ref.shape[1]
    relative = lists_ref[...] - base
    block_of = lax.broadcasted_iota(jnp.int32, (2 * prompts, positions), 1) // BLK
    kept = jnp.zeros((2 * prompts, positions), f32)
    for j in range(per_dev):
        flag = jnp.max(jnp.where(relative == j, 1.0, 0.0), axis=1, keepdims=True)
        kept = jnp.where(block_of == j, flag, kept)
    first = first_head_rows()
    lane = lax.broadcasted_iota(jnp.int32, (ROWS, HD), 1)
    unit = (
        lax.broadcasted_iota(jnp.int32, (16, HD), 0) == lax.broadcasted_iota(jnp.int32, (16, HD), 1)
    ).astype(bf16)
    for p in range(prompts):
        q = jnp.where(core == p % 2, q_own_ref[p // 2], q_sib_ref[p // 2])
        score = dot(two_head_queries(q, first), k_ref[p], 1, 1) * score_scale
        pair = [
            jnp.broadcast_to(kept[2 * p + h : 2 * p + h + 1], (GROUPS, positions)) for h in range(KV)
        ]
        keep = jnp.concatenate(pair * STEPS, axis=0) > 0.5
        score = jnp.where(keep, score, masked_score)
        top = jnp.max(score, axis=1, keepdims=True).astype(bf16).astype(f32)
        weight = jnp.where(keep, jnp.exp(score - top), 0.0).astype(bf16)
        total = jnp.sum(weight.astype(f32), axis=1, keepdims=True)
        summed = per_head(dot(weight, v_ref[p]), first)
        total_hi = total.astype(bf16).astype(f32)
        notes = jnp.where(
            lane == 0, top, jnp.where(lane == 1, total_hi, jnp.where(lane == 2, total - total_hi, 0.0))
        ).astype(bf16)
        notes = jnp.concatenate([notes, jnp.zeros((HD - ROWS, HD), bf16)], axis=0)
        out_ref[p, :ROWS, :] = summed.astype(bf16)
        out_ref[p, ROWS:, :] = dot(unit, notes, 1, 1).astype(bf16)


def combine_kernel(got_ref, q_ref, nk_ref, nv_ref, out_ref):
    holders = got_ref.shape[0]
    notes = got_ref[:, ROWS:, :].reshape(holders * 16, HD)
    row = lax.broadcasted_iota(jnp.int32, (holders * 16, HD), 0)
    col = lax.broadcasted_iota(jnp.int32, (holders * 16, HD), 1)
    pick = ((col == (row % 16) * holders + row // 16) & (row % 16 < 3)).astype(bf16)
    columns = dot(notes, pick, 0, 0)[:ROWS]
    tops = columns[:, :holders]
    totals = columns[:, holders : 2 * holders] + columns[:, 2 * holders : 3 * holders]
    first = first_head_rows()
    new_score = dot(two_head_queries(q_ref[...], first), nk_ref[...], 1, 1) * score_scale
    step = lax.broadcasted_iota(jnp.int32, new_score.shape, 0) // HQ
    token = lax.broadcasted_iota(jnp.int32, new_score.shape, 1)
    causal = token <= step
    new_score = jnp.where(causal, new_score, masked_score)
    top = jnp.maximum(
        jnp.max(tops, axis=1, keepdims=True), jnp.max(new_score, axis=1, keepdims=True)
    )
    share = jnp.exp(tops - top)
    new_weight = jnp.where(causal, jnp.exp(new_score - top), 0.0).astype(bf16)
    total = jnp.sum(share * totals, axis=1, keepdims=True) + jnp.sum(
        new_weight.astype(f32), axis=1, keepdims=True
    )
    summed = per_head(dot(new_weight, nv_ref[...]), first)
    for i in range(holders):
        summed = summed + share[:, i : i + 1] * got_ref[i, :ROWS, :].astype(f32)
    out_ref[...] = (summed / total).astype(bf16)


def project_kernel(where_ref, got_ref, own_ref, sib_ref, out_ref, wide_ref):
    core = where_ref[1]
    chips = got_ref.shape[0]
    wide_ref[...] = got_ref[...].reshape(chips * ROWS, HD).astype(f32)
    own = jnp.zeros((STEPS * chips, own_ref.shape[1]), f32)
    sib = jnp.zeros((STEPS * chips, own_ref.shape[1]), f32)
    for pair in range(HQ // 2):
        parts = []
        for h in (2 * pair, 2 * pair + 1):
            parts.append(
                jnp.concatenate(
                    [wide_ref[pl.ds(t * HQ + h, chips, stride=ROWS), :] for t in range(STEPS)], axis=0
                )
            )
        rows = jnp.concatenate(parts, axis=1).astype(bf16)
        at = slice(pair * 2 * HD, (pair + 1) * 2 * HD)
        own = own + dot(rows, own_ref[at, :])
        sib = sib + dot(rows, sib_ref[at, :])
    half = own_ref.shape[1]
    out_ref[:, :half] = jnp.where(core == 0, own, sib)
    out_ref[:, half:] = jnp.where(core == 0, sib, own)


def gate_up_kernel(
    where_ref, p0, p1, p2, p3, res_ref, gain_ref, g_own, g_sib, u_own, u_sib,
    out_ref, stream_ref, mine_ref, other_ref, square_ref,
):
    core = where_ref[1]
    half = g_own.shape[0]

    @pl.when(pl.program_id(0) == 0)
    def _():
        stream = res_ref[...].astype(f32) + ((p0[...] + p1[...]) + (p2[...] + p3[...]))
        stream_ref[...] = stream
        scaled = stream * gain_ref[0:1, :].astype(f32)
        mine_ref[...] = jnp.where(core == 0, scaled[:, :half], scaled[:, half:]).astype(bf16)
        other_ref[...] = jnp.where(core == 0, scaled[:, half:], scaled[:, :half]).astype(bf16)
        square = jnp.sum(stream * stream, axis=1, keepdims=True)
        square_hi = square.astype(bf16).astype(f32)
        tokens = square.shape[0]
        lane = lax.broadcasted_iota(jnp.int32, (tokens, HD), 1)
        notes = jnp.where(
            lane == 0, square_hi, jnp.where(lane == 1, square - square_hi, 0.0)
        ).astype(bf16)
        notes = jnp.concatenate([notes, jnp.zeros((HD - tokens, HD), bf16)], axis=0)
        unit = (
            lax.broadcasted_iota(jnp.int32, (16, HD), 0)
            == lax.broadcasted_iota(jnp.int32, (16, HD), 1)
        ).astype(bf16)
        square_ref[...] = dot(unit, notes, 1, 1).astype(bf16)

    mine = mine_ref[...]
    other = other_ref[...]
    tokens = mine.shape[0]
    gate = (dot(mine, g_own[...]) + dot(other, g_sib[...])).astype(bf16)
    up = (dot(mine, u_own[...]) + dot(other, u_sib[...])).astype(bf16)
    for k in range(out_ref.shape[0]):
        for part in range(2):
            at = slice((2 * k + part) * HD, (2 * k + part + 1) * HD)
            out_ref[k, part * tokens : (part + 1) * tokens, :] = gate[:, at]
            out_ref[k, (2 + part) * tokens : (3 + part) * tokens, :] = up[:, at]
        out_ref[k, 4 * tokens :, :] = square_ref[...]


def down_kernel(where_ref, got_ref, own_ref, sib_ref, out_ref, mine_ref, other_ref):
    core = where_ref[1]
    chips = got_ref.shape[0]
    tokens = mine_ref.shape[0]

    @pl.when(pl.program_id(0) == 0)
    def _():
        total = got_ref[0].astype(f32)
        for i in range(1, chips):
            total = total + got_ref[i].astype(f32)
        square = total[4 * tokens : 4 * tokens + 1, :] + total[4 * tokens + 1 : 4 * tokens + 2, :]
        scale_row = lax.rsqrt(square / D + norm_eps)
        row = lax.broadcasted_iota(jnp.int32, (tokens, HD), 0)
        col = lax.broadcasted_iota(jnp.int32, (tokens, HD), 1)
        scale = jnp.sum(jnp.where(row == col, scale_row, 0.0), axis=1, keepdims=True)
        halves = []
        for part in range(2):
            gate = total[part * tokens : (part + 1) * tokens] * scale
            up = total[(2 + part) * tokens : (3 + part) * tokens] * scale
            halves.append(gate / (1.0 + jnp.exp(-gate)) * up)
        mine_ref[...] = jnp.where(core == 0, halves[0], halves[1]).astype(bf16)
        other_ref[...] = jnp.where(core == 0, halves[1], halves[0]).astype(bf16)

    down = (dot(mine_ref[...], own_ref[...]) + dot(other_ref[...], sib_ref[...])).astype(bf16)
    width = out_ref.shape[2]
    for k in range(out_ref.shape[0]):
        out_ref[k] = down[:, k * width : (k + 1) * width]


def on_device(
    keys_cache,
    values_cache,
    keep_blocks,
    keep_count,
    queries,
    new_keys,
    new_values,
    residual_in,
    norm_gain,
    w_out,
    w_gate,
    w_up,
    w_down,
):
    holders = lax.axis_size("seq")
    chips = holders // 2
    holder = lax.axis_index("seq").astype(jnp.int32)
    core = holder % 2
    prompts, positions = keys_cache.shape[:2]
    per_dev = positions // BLK
    list_length = keep_blocks.shape[2]
    tokens = STEPS * chips
    width = residual_in.shape[2]
    where = jnp.stack([holder, core])
    smem = pl.BlockSpec(memory_space=pltpu.SMEM)
    vmem = pl.BlockSpec(memory_space=pltpu.VMEM)
    params = pltpu.CompilerParams(vmem_limit_bytes=40 * 1024 * 1024)

    same_core = [[2 * i + c for i in range(chips)] for c in range(2)]
    swap = [(i, i ^ 1) for i in range(holders)]

    def over_chips(x):
        return lax.all_to_all(
            x, "seq", split_axis=0, concat_axis=0, tiled=True, axis_index_groups=same_core
        )

    def to_all_chips(x):
        return over_chips(jnp.broadcast_to(x[None], (chips,) + x.shape))

    def sibling(x):
        return lax.ppermute(x, "seq", swap)

    def heads(x):
        return [x] + [lax.ppermute(x, "head", [(i, i ^ s) for i in range(4)]) for s in (1, 2, 3)]

    def parity(x, which):
        x = x.reshape(STEPS, chips, 2, width)
        return lax.dynamic_slice_in_dim(x, which, 1, 2).reshape(tokens, width)

    def in_order(own, sib):
        low = jnp.where(core == 0, own, sib)
        high = jnp.where(core == 0, sib, own)
        return jnp.concatenate([low, high], axis=1)

    q_rows = queries.reshape(ROWS, HD)
    q_own = to_all_chips(q_rows)
    q_sib = sibling(q_own)

    lists = jnp.where(
        jnp.arange(list_length)[None, None, :] < keep_count[:, :, None], keep_blocks, -1
    ).reshape(prompts * KV, list_length)

    batch = 4
    partial = pl.pallas_call(
        functools.partial(attend_kernel, per_dev),
        grid=(prompts // batch,),
        in_specs=[
            smem,
            pl.BlockSpec((batch * KV, list_length), lambda i: (i, 0)),
            pl.BlockSpec((batch // 2, ROWS, HD), lambda i: (i, 0, 0)),
            pl.BlockSpec((batch // 2, ROWS, HD), lambda i: (i, 0, 0)),
            pl.BlockSpec((batch, positions, KV * HD), lambda i: (i, 0, 0)),
            pl.BlockSpec((batch, positions, KV * HD), lambda i: (i, 0, 0)),
        ],
        out_specs=pl.BlockSpec((batch, PACK, HD), lambda i: (i, 0, 0)),
        out_shape=jax.ShapeDtypeStruct((prompts, PACK, HD), bf16),
        compiler_params=params,
        name="attend",
    )(where, lists, q_own, q_sib, keys_cache, values_cache)

    (w_out_s, w_gate_s, w_up_s, w_down_s, res_s, gain_s), _ = lax.optimization_barrier(
        ((w_out, w_gate, w_up, w_down, parity(residual_in, 1 - core), norm_gain), q_own)
    )
    w_out_sib = sibling(w_out_s)
    w_gate_sib = sibling(w_gate_s)
    w_up_sib = sibling(w_up_s)
    w_down_sib = sibling(w_down_s)
    extra = sibling(jnp.concatenate([res_s, jnp.broadcast_to(gain_s[None], (16, width))], axis=0))
    res = in_order(parity(residual_in, core), extra[:tokens])
    gain = in_order(jnp.broadcast_to(norm_gain[None], (16, width)), extra[tokens:])

    got = lax.all_to_all(partial, "seq", split_axis=0, concat_axis=0, tiled=True)
    pad = ((0, 16 - STEPS), (0, 0))
    attended = pl.pallas_call(
        combine_kernel,
        in_specs=[vmem] * 4,
        out_specs=vmem,
        out_shape=jax.ShapeDtypeStruct((ROWS, HD), bf16),
        compiler_params=params,
        name="combine",
    )(
        got,
        q_rows,
        jnp.pad(new_keys.reshape(STEPS, KV * HD), pad),
        jnp.pad(new_values.reshape(STEPS, KV * HD), pad),
    )

    all_attended = to_all_chips(attended)
    projected = pl.pallas_call(
        project_kernel,
        in_specs=[smem, vmem, vmem, vmem],
        out_specs=vmem,
        out_shape=jax.ShapeDtypeStruct((tokens, 2 * width), f32),
        scratch_shapes=[pltpu.VMEM((chips * ROWS, HD), f32)],
        compiler_params=params,
        name="project",
    )(where, all_attended, w_out, w_out_sib)
    parts = heads(projected)

    fixed = lambda *shape: pl.BlockSpec(shape, lambda i: (0,) * len(shape))
    hidden = w_gate.shape[1]
    per_step = 2
    gate_block = pl.BlockSpec((width, hidden // chips * per_step), lambda i: (0, i))
    shares, stream = pl.pallas_call(
        gate_up_kernel,
        grid=(chips // per_step,),
        in_specs=[smem]
        + [fixed(tokens, 2 * width)] * 5
        + [fixed(16, 2 * width)]
        + [gate_block] * 4,
        out_specs=[
            pl.BlockSpec((per_step, 4 * tokens + 16, HD), lambda i: (i, 0, 0)),
            fixed(tokens, 2 * width),
        ],
        out_shape=[
            jax.ShapeDtypeStruct((chips, 4 * tokens + 16, HD), bf16),
            jax.ShapeDtypeStruct((tokens, 2 * width), f32),
        ],
        scratch_shapes=[
            pltpu.VMEM((tokens, width), bf16),
            pltpu.VMEM((tokens, width), bf16),
            pltpu.VMEM((16, HD), bf16),
        ],
        compiler_params=params,
        name="gate_up",
    )(where, *parts, res, gain, w_gate, w_gate_sib, w_up, w_up_sib)

    got_shares = over_chips(shares)
    rows = w_down.shape[0]
    down_step = 4
    down_block = pl.BlockSpec((rows, 2 * width * down_step), lambda i: (0, i))
    down = pl.pallas_call(
        down_kernel,
        grid=(chips // down_step,),
        in_specs=[smem, fixed(chips, 4 * tokens + 16, HD), down_block, down_block],
        out_specs=pl.BlockSpec((down_step, tokens, 2 * width), lambda i: (i, 0, 0)),
        out_shape=jax.ShapeDtypeStruct((chips, tokens, 2 * width), bf16),
        scratch_shapes=[pltpu.VMEM((tokens, rows), bf16), pltpu.VMEM((tokens, rows), bf16)],
        compiler_params=params,
        name="down",
    )(where, got_shares, w_down, w_down_sib)

    lowered = jnp.sum(over_chips(down).astype(f32), axis=0)
    l0, l1, l2, l3 = heads(lowered)
    final = (stream + ((l0 + l1) + (l2 + l3))).astype(bf16)
    low, high = final[:, :width], final[:, width:]
    keep = jnp.where(core == 0, low, high)
    come = sibling(jnp.where(core == 0, high, low))
    even = jnp.where(core == 0, keep, come).reshape(STEPS, chips, 1, width)
    odd = jnp.where(core == 0, come, keep).reshape(STEPS, chips, 1, width)
    layer_out = jnp.concatenate([even, odd], axis=2).reshape(STEPS, holders, width)
    return (attended.reshape(STEPS, 1, HQ * HD), layer_out)


def solution(mesh):
    placed = (
        P(None, "seq", "head"),
        P(None, "seq", "head"),
        P(None, "head", None),
        P(None, "head"),
        P(None, "seq", "head"),
        P(None, "seq", "head"),
        P(None, "seq", "head"),
        P(None, None, "seq"),
        P("seq"),
        P("head", "seq"),
        P("seq", "head"),
        P("seq", "head"),
        P(("head", "seq"), None),
    )
    return jax.shard_map(
        on_device,
        mesh=mesh,
        in_specs=placed,
        out_specs=(P(None, "seq", "head"), P(None, None, "seq")),
        check_vma=False,
    )
```

```python
import functools

import jax
import jax.numpy as jnp
from jax import lax
from jax.experimental import pallas as pl
from jax.experimental.pallas import tpu as pltpu
from jax.sharding import PartitionSpec as P

D = 8192
H = 64
KVH = 8
HD = 128
BLK = 64
CAP = 4
GROUPS = H // KVH

masked_score = -1e30
norm_eps = 1e-06
score_scale = HD ** (-0.5)

f32 = jnp.float32
bf16 = jnp.bfloat16
MIB = 1 << 20

STEPS = 3
KV = 2
HQ = KV * GROUPS
ROWS = STEPS * HQ
PACK = ROWS + 16


def dot(a, b, ca=1, cb=0):
    return lax.dot_general(a, b, (((ca,), (cb,)), ((), ())), preferred_element_type=f32)


def first_head_rows():
    rows = lax.broadcasted_iota(jnp.int32, (ROWS, 1), 0)
    return (rows // GROUPS) % KV == 0


def two_head_queries(q, first):
    zero = jnp.zeros_like(q)
    return jnp.concatenate([jnp.where(first, q, zero), jnp.where(first, zero, q)], axis=1)


def per_head(values, first):
    return jnp.where(first, values[:, :HD], values[:, HD:])


def pack_prompt(prompt, codes, k_ref, v_ref, packed_ref, sem):
    half = CAP * BLK
    for h in range(KV):
        lanes = pl.ds(h * HD, HD)
        for s in range(CAP):
            at = pl.multiple_of(((codes[h] >> (3 * s)) & 7) * BLK, BLK)
            for part, cache_ref in enumerate((k_ref, v_ref)):
                pltpu.make_async_copy(
                    cache_ref.at[prompt, pl.ds(at, BLK), lanes],
                    packed_ref.at[pl.ds(part * half + s * BLK, BLK), lanes],
                    sem,
                ).start()


def gather_kernel(
    where_ref, count_ref, lists_ref, k_ref, v_ref, out_ref, codes_ref,
    wide_ref, scalar_ref, packed_ref, list_sem, in_sems, out_sems,
):
    core = where_ref[1]
    per_dev = k_ref.shape[1] // BLK
    base = where_ref[0] * per_dev
    sib_base = (where_ref[0] + 1 - 2 * core) * per_dev
    lists = lists_ref[...]
    lane = lax.broadcasted_iota(jnp.int32, lists.shape, 2)
    valid = (lists > 0) | (lane == 0)
    before = jnp.sum(jnp.where(valid & (lists < base), 1.0, 0.0), axis=2, keepdims=True)
    local = lists - base
    mine = valid & (local >= 0) & (local < per_dev)
    theirs = valid & (lists >= sib_base) & (lists < sib_base + per_dev)
    rank = jnp.clip(lane - before.astype(jnp.int32), 0, CAP - 1)
    share = jnp.where(mine, jnp.left_shift(local, 3 * rank) + (1 << 12), 0)
    share = share + jnp.where(theirs, 1 << 15, 0)
    code = jnp.sum(share.astype(f32), axis=2, keepdims=True).astype(jnp.int32)
    spot = lax.broadcasted_iota(jnp.int32, lists.shape, 0) * KV + lax.broadcasted_iota(
        jnp.int32, lists.shape, 1
    )
    wide_ref[...] = jnp.sum(jnp.sum(jnp.where(lane == spot, code, 0), axis=0), axis=0, keepdims=True)
    listed = pltpu.make_async_copy(wide_ref, scalar_ref, list_sem)
    listed.start()
    listed.wait()

    def code_of(prompt, h):
        return jnp.where(count_ref[h, prompt] > 0, scalar_ref[0, prompt * KV + h], 0)

    chips = packed_ref.shape[0]
    groups = in_sems.shape[0]
    size = chips // groups
    for g in range(groups):

        def one(i, carry):
            chip = g * size + i
            prompt = chip * 2 + 1 - core
            codes = [code_of(prompt, h) for h in range(KV)]
            pack_prompt(prompt, codes, k_ref, v_ref, packed_ref.at[chip], in_sems.at[g])
            for h in range(KV):
                codes_ref[chip * KV + h] = code_of(chip * 2 + core, h)
            return carry

        lax.fori_loop(0, size, one, 0)
    leaving = []
    for g in range(groups):
        at = pl.ds(g * size, size)
        pltpu.make_async_copy(packed_ref.at[at], packed_ref.at[at], in_sems.at[g]).wait()
        leaving.append(pltpu.make_async_copy(packed_ref.at[at], out_ref.at[at], out_sems.at[g]))
        leaving[-1].start()
    for copy in leaving:
        copy.wait()


def attend_kernel(
    where_ref, codes_ref, q_ref, k_ref, v_ref, sib_hbm, out_ref, own_ref, sib_ref, own_sems, sib_sems
):
    core = where_ref[1]
    half = CAP * BLK
    chips = q_ref.shape[0]
    groups = own_sems.shape[0]
    size = chips // groups
    first = first_head_rows()
    lane = lax.broadcasted_iota(jnp.int32, (ROWS, HD), 1)
    slot_lane = lax.broadcasted_iota(jnp.int32, (ROWS, half), 1)
    unit = (
        lax.broadcasted_iota(jnp.int32, (16, HD), 0) == lax.broadcasted_iota(jnp.int32, (16, HD), 1)
    ).astype(bf16)

    def from_sib(g):
        at = pl.ds(g * size, size)
        return pltpu.make_async_copy(sib_hbm.at[at], sib_ref.at[at], sib_sems.at[g])

    def fetch(g):
        from_sib(g).start()

        def one(i, carry):
            chip = g * size + i
            codes = [codes_ref[chip * KV + h] for h in range(KV)]
            pack_prompt(chip * 2 + core, codes, k_ref, v_ref, own_ref.at[chip], own_sems.at[g])
            return carry

        lax.fori_loop(0, size, one, 0)

    def score_of(chip):
        queries = two_head_queries(q_ref[chip], first)
        scores, keeps = [], []
        for shift, blocks_ref in ((12, own_ref), (15, sib_ref)):
            ends = [((codes_ref[chip * KV + h] >> shift) & 7) * BLK for h in range(KV)]
            keeps.append(slot_lane < jnp.where(first, ends[0], ends[1]))
            scores.append(dot(queries, blocks_ref[chip, :half, :], 1, 1))
        return jnp.concatenate(keeps, axis=1), jnp.concatenate(scores, axis=1)

    def weigh(keep, score):
        score = jnp.where(keep, score * score_scale, masked_score)
        top = jnp.max(score, axis=1, keepdims=True).astype(bf16).astype(f32)
        weight = jnp.where(keep, jnp.exp(score - top), 0.0).astype(bf16)
        return top, weight, jnp.sum(weight.astype(f32), axis=1, keepdims=True)

    def store(chip, top, weight, total):
        summed = per_head(
            dot(weight[:, :half], own_ref[chip, half:, :])
            + dot(weight[:, half:], sib_ref[chip, half:, :]),
            first,
        )
        total_hi = total.astype(bf16).astype(f32)
        notes = jnp.where(
            lane == 0, top, jnp.where(lane == 1, total_hi, jnp.where(lane == 2, total - total_hi, 0.0))
        ).astype(bf16)
        notes = jnp.concatenate([notes, jnp.zeros((HD - ROWS, HD), bf16)], axis=0)
        out_ref[chip, :ROWS, :] = summed.astype(bf16)
        out_ref[chip, ROWS:, :] = dot(unit, notes, 1, 1).astype(bf16)

    fetch(0)
    for g in range(groups):
        if g + 1 < groups:
            fetch(g + 1)
        at = pl.ds(g * size, size)
        pltpu.make_async_copy(own_ref.at[at], own_ref.at[at], own_sems.at[g]).wait()
        from_sib(g).wait()
        chips_now = range(g * size, (g + 1) * size)
        scored = [score_of(chip) for chip in chips_now]
        weighed = [weigh(*each) for each in scored]
        for chip, each in zip(chips_now, weighed):
            store(chip, *each)


def combine_kernel(got_ref, q_ref, nk_ref, nv_ref, out_ref):
    holders = got_ref.shape[0]
    notes = got_ref[:, ROWS:, :].reshape(holders * 16, HD)
    row = lax.broadcasted_iota(jnp.int32, (holders * 16, HD), 0)
    col = lax.broadcasted_iota(jnp.int32, (holders * 16, HD), 1)
    pick = ((col == (row % 16) * holders + row // 16) & (row % 16 < 3)).astype(bf16)
    columns = dot(notes, pick, 0, 0)[:ROWS]
    tops = columns[:, :holders]
    totals = columns[:, holders : 2 * holders] + columns[:, 2 * holders : 3 * holders]
    first = first_head_rows()
    new_score = dot(two_head_queries(q_ref[...], first), nk_ref[...], 1, 1) * score_scale
    step = lax.broadcasted_iota(jnp.int32, new_score.shape, 0) // HQ
    token = lax.broadcasted_iota(jnp.int32, new_score.shape, 1)
    causal = token <= step
    new_score = jnp.where(causal, new_score, masked_score)
    top = jnp.maximum(
        jnp.max(tops, axis=1, keepdims=True), jnp.max(new_score, axis=1, keepdims=True)
    )
    share = jnp.exp(tops - top)
    new_weight = jnp.where(causal, jnp.exp(new_score - top), 0.0).astype(bf16)
    total = jnp.sum(share * totals, axis=1, keepdims=True) + jnp.sum(
        new_weight.astype(f32), axis=1, keepdims=True
    )
    summed = per_head(dot(new_weight, nv_ref[...]), first)
    for i in range(holders):
        summed = summed + share[:, i : i + 1] * got_ref[i, :ROWS, :].astype(f32)
    out_ref[...] = (summed / total).astype(bf16)


def project_kernel(where_ref, got_ref, own_ref, sib_ref, out_ref, wide_ref):
    core = where_ref[1]
    chips = got_ref.shape[0]
    wide_ref[...] = got_ref[...].reshape(chips * ROWS, HD).astype(f32)
    own = jnp.zeros((STEPS * chips, own_ref.shape[1]), f32)
    sib = jnp.zeros((STEPS * chips, own_ref.shape[1]), f32)
    for pair in range(HQ // 2):
        parts = []
        for h in (2 * pair, 2 * pair + 1):
            parts.append(
                jnp.concatenate(
                    [wide_ref[pl.ds(t * HQ + h, chips, stride=ROWS), :] for t in range(STEPS)], axis=0
                )
            )
        rows = jnp.concatenate(parts, axis=1).astype(bf16)
        at = slice(pair * 2 * HD, (pair + 1) * 2 * HD)
        own = own + dot(rows, own_ref[at, :])
        sib = sib + dot(rows, sib_ref[at, :])
    half = own_ref.shape[1]
    out_ref[:, :half] = jnp.where(core == 0, own, sib)
    out_ref[:, half:] = jnp.where(core == 0, sib, own)


def gate_up_kernel(
    where_ref, p0, p1, p2, p3, res_ref, gain_ref, g_own, g_sib, u_own, u_sib, out_ref, stream_ref
):
    core = where_ref[1]
    half = g_own.shape[0]
    chips = out_ref.shape[0]
    stream = res_ref[...].astype(f32) + ((p0[...] + p1[...]) + (p2[...] + p3[...]))
    stream_ref[...] = stream
    scaled = stream * gain_ref[0:1, :].astype(f32)
    mine = jnp.where(core == 0, scaled[:, :half], scaled[:, half:]).astype(bf16)
    other = jnp.where(core == 0, scaled[:, half:], scaled[:, :half]).astype(bf16)
    square = jnp.sum(stream * stream, axis=1, keepdims=True)
    square_hi = square.astype(bf16).astype(f32)
    tokens = square.shape[0]
    lane = lax.broadcasted_iota(jnp.int32, (tokens, HD), 1)
    notes = jnp.where(
        lane == 0, square_hi, jnp.where(lane == 1, square - square_hi, 0.0)
    ).astype(bf16)
    notes = jnp.concatenate([notes, jnp.zeros((HD - tokens, HD), bf16)], axis=0)
    unit = (
        lax.broadcasted_iota(jnp.int32, (16, HD), 0) == lax.broadcasted_iota(jnp.int32, (16, HD), 1)
    ).astype(bf16)
    squares = dot(unit, notes, 1, 1).astype(bf16)
    wide = g_own.shape[1] // chips

    def store(k, gate, up):
        for part in range(2):
            at = slice(part * HD, (part + 1) * HD)
            out_ref[k, part * tokens : (part + 1) * tokens, :] = gate[:, at]
            out_ref[k, (2 + part) * tokens : (3 + part) * tokens, :] = up[:, at]
        out_ref[k, 4 * tokens :, :] = squares

    ready = None
    for k in range(chips):
        at = slice(k * wide, (k + 1) * wide)
        gate = dot(mine, g_own[:, at]) + dot(other, g_sib[:, at])
        up = dot(mine, u_own[:, at]) + dot(other, u_sib[:, at])
        if ready:
            store(*ready)
        ready = k, gate.astype(bf16), up.astype(bf16)
    store(*ready)


def down_kernel(where_ref, got_ref, own_ref, sib_ref, out_ref):
    core = where_ref[1]
    chips, tokens, width = out_ref.shape
    total = got_ref[0].astype(f32)
    for i in range(1, chips):
        total = total + got_ref[i].astype(f32)
    square = total[4 * tokens : 4 * tokens + 1, :] + total[4 * tokens + 1 : 4 * tokens + 2, :]
    scale_row = lax.rsqrt(square / D + norm_eps)
    row = lax.broadcasted_iota(jnp.int32, (tokens, HD), 0)
    col = lax.broadcasted_iota(jnp.int32, (tokens, HD), 1)
    scale = jnp.sum(jnp.where(row == col, scale_row, 0.0), axis=1, keepdims=True)
    halves = []
    for part in range(2):
        gate = total[part * tokens : (part + 1) * tokens] * scale
        up = total[(2 + part) * tokens : (3 + part) * tokens] * scale
        halves.append(gate / (1.0 + jnp.exp(-gate)) * up)
    mine = jnp.where(core == 0, halves[0], halves[1]).astype(bf16)
    other = jnp.where(core == 0, halves[1], halves[0]).astype(bf16)
    rows = jnp.concatenate([mine, other], axis=1)
    for k in range(chips):
        at = slice(k * width, (k + 1) * width)
        out_ref[k] = dot(rows, jnp.concatenate([own_ref[:, at], sib_ref[:, at]], axis=0)).astype(bf16)


def on_device(
    keys_cache,
    values_cache,
    keep_blocks,
    keep_count,
    queries,
    new_keys,
    new_values,
    residual_in,
    norm_gain,
    w_out,
    w_gate,
    w_up,
    w_down,
):
    holders = lax.axis_size("seq")
    chips = holders // 2
    holder = lax.axis_index("seq").astype(jnp.int32)
    core = holder % 2
    prompts, positions = keys_cache.shape[:2]
    per_dev = positions // BLK
    list_length = keep_blocks.shape[2]
    tokens = STEPS * chips
    width = residual_in.shape[2]
    where = jnp.stack([holder, core])
    smem = pl.BlockSpec(memory_space=pltpu.SMEM)
    vmem = pl.BlockSpec(memory_space=pltpu.VMEM)
    hbm = pl.BlockSpec(memory_space=pltpu.HBM)
    params = pltpu.CompilerParams(vmem_limit_bytes=24 * MIB)

    same_core = [[2 * i + c for i in range(chips)] for c in range(2)]
    swap = [(i, i ^ 1) for i in range(holders)]

    def over_chips(x):
        return lax.all_to_all(
            x, "seq", split_axis=0, concat_axis=0, tiled=True, axis_index_groups=same_core
        )

    def to_all_chips(x):
        return over_chips(jnp.broadcast_to(x[None], (chips,) + x.shape))

    def sibling(x):
        return lax.ppermute(x, "seq", swap)

    def heads(x):
        return [x] + [lax.ppermute(x, "head", [(i, i ^ s) for i in range(4)]) for s in (1, 2, 3)]

    def parity(x, which):
        x = x.reshape(STEPS, chips, 2, width)
        return lax.dynamic_slice_in_dim(x, which, 1, 2).reshape(tokens, width)

    def in_order(own, sib):
        low = jnp.where(core == 0, own, sib)
        high = jnp.where(core == 0, sib, own)
        return jnp.concatenate([low, high], axis=1)

    q_rows = queries.reshape(ROWS, HD)
    q_own = to_all_chips(q_rows)

    half = CAP * BLK
    tile = (chips, 2 * half, KV * HD)
    groups = 4
    dma = pltpu.SemaphoreType.DMA
    to_sib, codes = pl.pallas_call(
        gather_kernel,
        in_specs=[smem, smem, vmem, hbm, hbm],
        out_specs=[hbm, smem],
        out_shape=[jax.ShapeDtypeStruct(tile, bf16), jax.ShapeDtypeStruct((chips * KV,), jnp.int32)],
        scratch_shapes=[
            pltpu.VMEM((1, list_length), jnp.int32),
            pltpu.SMEM((1, list_length), jnp.int32),
            pltpu.VMEM(tile, bf16),
            dma,
            dma((groups,)),
            dma((groups,)),
        ],
        compiler_params=pltpu.CompilerParams(vmem_limit_bytes=50 * MIB),
        name="gather",
    )(where, keep_count.T, keep_blocks, keys_cache, values_cache)
    sib_packed = sibling(to_sib)
    partial = pl.pallas_call(
        attend_kernel,
        in_specs=[smem, smem, vmem, hbm, hbm, pl.BlockSpec(memory_space=pl.ANY)],
        out_specs=vmem,
        out_shape=jax.ShapeDtypeStruct((chips, PACK, HD), bf16),
        scratch_shapes=[pltpu.VMEM(tile, bf16)] * 2 + [dma((groups,))] * 2,
        compiler_params=pltpu.CompilerParams(vmem_limit_bytes=50 * MIB),
        name="attend",
    )(where, codes, q_own, keys_cache, values_cache, sib_packed)

    (w_out_s, w_gate_s, w_up_s, w_down_s, res_s, gain_s), _ = lax.optimization_barrier(
        ((w_out, w_gate, w_up, w_down, parity(residual_in, 1 - core), norm_gain), q_own)
    )
    w_out_sib = sibling(w_out_s)
    w_gate_sib = sibling(w_gate_s)
    w_up_sib = sibling(w_up_s)
    w_down_sib = sibling(w_down_s)
    extra = sibling(jnp.concatenate([res_s, jnp.broadcast_to(gain_s[None], (16, width))], axis=0))
    res = in_order(parity(residual_in, core), extra[:tokens])
    gain = in_order(jnp.broadcast_to(norm_gain[None], (16, width)), extra[tokens:])

    got = over_chips(partial)
    pad = ((0, 16 - STEPS), (0, 0))
    attended = pl.pallas_call(
        combine_kernel,
        in_specs=[vmem] * 4,
        out_specs=vmem,
        out_shape=jax.ShapeDtypeStruct((ROWS, HD), bf16),
        compiler_params=params,
        name="combine",
    )(
        got,
        q_rows,
        jnp.pad(new_keys.reshape(STEPS, KV * HD), pad),
        jnp.pad(new_values.reshape(STEPS, KV * HD), pad),
    )

    all_attended = to_all_chips(attended)
    projected = pl.pallas_call(
        project_kernel,
        in_specs=[smem, vmem, vmem, vmem],
        out_specs=vmem,
        out_shape=jax.ShapeDtypeStruct((tokens, 2 * width), f32),
        scratch_shapes=[pltpu.VMEM((chips * ROWS, HD), f32)],
        compiler_params=params,
        name="project",
    )(where, all_attended, w_out, w_out_sib)
    parts = heads(projected)

    shares, stream = pl.pallas_call(
        gate_up_kernel,
        in_specs=[smem] + [vmem] * 10,
        out_specs=[vmem, vmem],
        out_shape=[
            jax.ShapeDtypeStruct((chips, 4 * tokens + 16, HD), bf16),
            jax.ShapeDtypeStruct((tokens, 2 * width), f32),
        ],
        compiler_params=params,
        name="gate_up",
    )(where, *parts, res, gain, w_gate, w_gate_sib, w_up, w_up_sib)

    got_shares = over_chips(shares)
    down = pl.pallas_call(
        down_kernel,
        in_specs=[smem, vmem, vmem, vmem],
        out_specs=vmem,
        out_shape=jax.ShapeDtypeStruct((chips, tokens, 2 * width), bf16),
        compiler_params=params,
        name="down",
    )(where, got_shares, w_down, w_down_sib)

    lowered = jnp.sum(over_chips(down).astype(f32), axis=0)
    l0, l1, l2, l3 = heads(lowered)
    final = (stream + ((l0 + l1) + (l2 + l3))).astype(bf16)
    low, high = final[:, :width], final[:, width:]
    keep = jnp.where(core == 0, low, high)
    come = sibling(jnp.where(core == 0, high, low))
    even = jnp.where(core == 0, keep, come).reshape(STEPS, chips, 1, width)
    odd = jnp.where(core == 0, come, keep).reshape(STEPS, chips, 1, width)
    layer_out = jnp.concatenate([even, odd], axis=2).reshape(STEPS, holders, width)
    return (attended.reshape(STEPS, 1, HQ * HD), layer_out)


def solution(mesh):
    placed = (
        P(None, "seq", "head"),
        P(None, "seq", "head"),
        P(None, "head", None),
        P(None, "head"),
        P(None, "seq", "head"),
        P(None, "seq", "head"),
        P(None, "seq", "head"),
        P(None, None, "seq"),
        P("seq"),
        P("head", "seq"),
        P("seq", "head"),
        P("seq", "head"),
        P(("head", "seq"), None),
    )
    return jax.shard_map(
        on_device,
        mesh=mesh,
        in_specs=placed,
        out_specs=(P(None, "seq", "head"), P(None, None, "seq")),
        check_vma=False,
    )
```

```python
import functools

import jax
import jax.numpy as jnp
from jax import lax
from jax.experimental import pallas as pl
from jax.experimental.pallas import tpu as pltpu
from jax.sharding import PartitionSpec as P

D = 8192
H = 64
KVH = 8
HD = 128
BLK = 64
CAP = 4
GROUPS = H // KVH

masked_score = -1e30
norm_eps = 1e-06
score_scale = HD ** (-0.5)

f32 = jnp.float32
bf16 = jnp.bfloat16
MIB = 1 << 20

STEPS = 3
KV = 2
HQ = KV * GROUPS
ROWS = STEPS * HQ
PACK = ROWS + 16


def dot(a, b, ca=1, cb=0):
    return lax.dot_general(a, b, (((ca,), (cb,)), ((), ())), preferred_element_type=f32)


def first_head_rows():
    rows = lax.broadcasted_iota(jnp.int32, (ROWS, 1), 0)
    return (rows // GROUPS) % KV == 0


def two_head_queries(q, first):
    zero = jnp.zeros_like(q)
    return jnp.concatenate([jnp.where(first, q, zero), jnp.where(first, zero, q)], axis=1)


def per_head(values, first):
    return jnp.where(first, values[:, :HD], values[:, HD:])


def pack_prompt(prompt, codes, k_ref, v_ref, packed_ref, sem):
    half = CAP * BLK
    for h in range(KV):
        lanes = pl.ds(h * HD, HD)
        for s in range(CAP):
            at = pl.multiple_of(((codes[h] >> (3 * s)) & 7) * BLK, BLK)
            for part, cache_ref in enumerate((k_ref, v_ref)):
                pltpu.make_async_copy(
                    cache_ref.at[prompt, pl.ds(at, BLK), lanes],
                    packed_ref.at[pl.ds(part * half + s * BLK, BLK), lanes],
                    sem,
                ).start()


def gather_kernel(
    where_ref, count_ref, lists_ref, q_ref, k_ref, v_ref, out_ref, q_out, codes_ref,
    wide_ref, scalar_ref, packed_ref, list_sem, q_sems, in_sems, out_sems,
):
    spread = [
        pltpu.make_async_copy(q_ref, q_out.at[i], q_sems.at[i]) for i in range(q_out.shape[0])
    ]
    for copy in spread:
        copy.start()
    core = where_ref[1]
    per_dev = k_ref.shape[1] // BLK
    base = where_ref[0] * per_dev
    sib_base = (where_ref[0] + 1 - 2 * core) * per_dev
    lists = lists_ref[...]
    lane = lax.broadcasted_iota(jnp.int32, lists.shape, 2)
    valid = (lists > 0) | (lane == 0)
    before = jnp.sum(jnp.where(valid & (lists < base), 1.0, 0.0), axis=2, keepdims=True)
    local = lists - base
    mine = valid & (local >= 0) & (local < per_dev)
    theirs = valid & (lists >= sib_base) & (lists < sib_base + per_dev)
    rank = jnp.clip(lane - before.astype(jnp.int32), 0, CAP - 1)
    share = jnp.where(mine, jnp.left_shift(local, 3 * rank) + (1 << 12), 0)
    share = share + jnp.where(theirs, 1 << 15, 0)
    code = jnp.sum(share.astype(f32), axis=2, keepdims=True).astype(jnp.int32)
    spot = lax.broadcasted_iota(jnp.int32, lists.shape, 0) * KV + lax.broadcasted_iota(
        jnp.int32, lists.shape, 1
    )
    wide_ref[...] = jnp.sum(jnp.sum(jnp.where(lane == spot, code, 0), axis=0), axis=0, keepdims=True)
    listed = pltpu.make_async_copy(wide_ref, scalar_ref, list_sem)
    listed.start()
    listed.wait()

    def code_of(prompt, h):
        return jnp.where(count_ref[h, prompt] > 0, scalar_ref[0, prompt * KV + h], 0)

    chips = packed_ref.shape[0]
    groups = in_sems.shape[0]
    size = chips // groups
    for g in range(groups):

        def one(i, carry):
            chip = g * size + i
            prompt = chip * 2 + 1 - core
            codes = [code_of(prompt, h) for h in range(KV)]
            pack_prompt(prompt, codes, k_ref, v_ref, packed_ref.at[chip], in_sems.at[g])
            for h in range(KV):
                codes_ref[chip * KV + h] = code_of(chip * 2 + core, h)
            return carry

        lax.fori_loop(0, size, one, 0)
    leaving = []
    for g in range(groups):
        at = pl.ds(g * size, size)
        pltpu.make_async_copy(packed_ref.at[at], packed_ref.at[at], in_sems.at[g]).wait()
        leaving.append(pltpu.make_async_copy(packed_ref.at[at], out_ref.at[at], out_sems.at[g]))
        leaving[-1].start()
    for copy in leaving + spread:
        copy.wait()


def attend_kernel(
    where_ref, codes_ref, q_ref, k_ref, v_ref, sib_hbm, out_ref, own_ref, sib_ref, own_sems, sib_sems
):
    core = where_ref[1]
    half = CAP * BLK
    chips = q_ref.shape[0]
    groups = own_sems.shape[0]
    size = chips // groups
    first = first_head_rows()
    lane = lax.broadcasted_iota(jnp.int32, (ROWS, HD), 1)
    slot_lane = lax.broadcasted_iota(jnp.int32, (ROWS, half), 1)
    unit = (
        lax.broadcasted_iota(jnp.int32, (16, HD), 0) == lax.broadcasted_iota(jnp.int32, (16, HD), 1)
    ).astype(bf16)

    def from_sib(g):
        at = pl.ds(g * size, size)
        return pltpu.make_async_copy(sib_hbm.at[at], sib_ref.at[at], sib_sems.at[g])

    def fetch(g):
        from_sib(g).start()

        def one(i, carry):
            chip = g * size + i
            codes = [codes_ref[chip * KV + h] for h in range(KV)]
            pack_prompt(chip * 2 + core, codes, k_ref, v_ref, own_ref.at[chip], own_sems.at[g])
            return carry

        lax.fori_loop(0, size, one, 0)

    def score_of(chip):
        queries = two_head_queries(q_ref[chip], first)
        scores, keeps = [], []
        for shift, blocks_ref in ((12, own_ref), (15, sib_ref)):
            ends = [((codes_ref[chip * KV + h] >> shift) & 7) * BLK for h in range(KV)]
            keeps.append(slot_lane < jnp.where(first, ends[0], ends[1]))
            scores.append(dot(queries, blocks_ref[chip, :half, :], 1, 1))
        return jnp.concatenate(keeps, axis=1), jnp.concatenate(scores, axis=1)

    def weigh(keep, score):
        score = jnp.where(keep, score * score_scale, masked_score)
        top = jnp.max(score, axis=1, keepdims=True).astype(bf16).astype(f32)
        weight = jnp.where(keep, jnp.exp(score - top), 0.0).astype(bf16)
        return top, weight, jnp.sum(weight.astype(f32), axis=1, keepdims=True)

    def store(chip, top, weight, total):
        summed = per_head(
            dot(weight[:, :half], own_ref[chip, half:, :])
            + dot(weight[:, half:], sib_ref[chip, half:, :]),
            first,
        )
        total_hi = total.astype(bf16).astype(f32)
        notes = jnp.where(
            lane == 0, top, jnp.where(lane == 1, total_hi, jnp.where(lane == 2, total - total_hi, 0.0))
        ).astype(bf16)
        notes = jnp.concatenate([notes, jnp.zeros((HD - ROWS, HD), bf16)], axis=0)
        out_ref[chip, :ROWS, :] = summed.astype(bf16)
        out_ref[chip, ROWS:, :] = dot(unit, notes, 1, 1).astype(bf16)

    fetch(0)
    for g in range(groups):
        if g + 1 < groups:
            fetch(g + 1)
        at = pl.ds(g * size, size)
        pltpu.make_async_copy(own_ref.at[at], own_ref.at[at], own_sems.at[g]).wait()
        from_sib(g).wait()
        chips_now = range(g * size, (g + 1) * size)
        scored = [score_of(chip) for chip in chips_now]
        weighed = [weigh(*each) for each in scored]
        for chip, each in zip(chips_now, weighed):
            store(chip, *each)


def combine_kernel(got_ref, q_ref, nk_ref, nv_ref, out_ref):
    holders = got_ref.shape[0]
    notes = got_ref[:, ROWS:, :].reshape(holders * 16, HD)
    row = lax.broadcasted_iota(jnp.int32, (holders * 16, HD), 0)
    col = lax.broadcasted_iota(jnp.int32, (holders * 16, HD), 1)
    pick = ((col == (row % 16) * holders + row // 16) & (row % 16 < 3)).astype(bf16)
    columns = dot(notes, pick, 0, 0)[:ROWS]
    tops = columns[:, :holders]
    totals = columns[:, holders : 2 * holders] + columns[:, 2 * holders : 3 * holders]
    first = first_head_rows()
    new_score = dot(two_head_queries(q_ref[...], first), nk_ref[...], 1, 1) * score_scale
    step = lax.broadcasted_iota(jnp.int32, new_score.shape, 0) // HQ
    token = lax.broadcasted_iota(jnp.int32, new_score.shape, 1)
    causal = token <= step
    new_score = jnp.where(causal, new_score, masked_score)
    top = jnp.maximum(
        jnp.max(tops, axis=1, keepdims=True), jnp.max(new_score, axis=1, keepdims=True)
    )
    share = jnp.exp(tops - top)
    new_weight = jnp.where(causal, jnp.exp(new_score - top), 0.0).astype(bf16)
    total = jnp.sum(share * totals, axis=1, keepdims=True) + jnp.sum(
        new_weight.astype(f32), axis=1, keepdims=True
    )
    summed = per_head(dot(new_weight, nv_ref[...]), first)
    for i in range(holders):
        summed = summed + share[:, i : i + 1] * got_ref[i, :ROWS, :].astype(f32)
    out_ref[...] = (summed / total).astype(bf16)


def project_kernel(where_ref, got_ref, own_ref, sib_ref, out_ref, wide_ref):
    core = where_ref[1]
    chips = got_ref.shape[0]
    wide_ref[...] = got_ref[...].reshape(chips * ROWS, HD).astype(f32)
    own = jnp.zeros((STEPS * chips, own_ref.shape[1]), f32)
    sib = jnp.zeros((STEPS * chips, own_ref.shape[1]), f32)
    for pair in range(HQ // 2):
        parts = []
        for h in (2 * pair, 2 * pair + 1):
            parts.append(
                jnp.concatenate(
                    [wide_ref[pl.ds(t * HQ + h, chips, stride=ROWS), :] for t in range(STEPS)], axis=0
                )
            )
        rows = jnp.concatenate(parts, axis=1).astype(bf16)
        at = slice(pair * 2 * HD, (pair + 1) * 2 * HD)
        own = own + dot(rows, own_ref[at, :])
        sib = sib + dot(rows, sib_ref[at, :])
    half = own_ref.shape[1]
    out_ref[:, :half] = jnp.where(core == 0, own, sib)
    out_ref[:, half:] = jnp.where(core == 0, sib, own)


def gate_up_kernel(
    where_ref, p0, p1, p2, p3, res_ref, gain_ref, g_own_hbm, u_own_hbm, g_sib_hbm, u_sib_hbm,
    d_own_hbm, d_sib_hbm, out_ref, stream_ref, d_own_ref, d_sib_ref, g_own, u_own, g_sib, u_sib,
    part_sems, whole_sems,
):
    core = where_ref[1]
    parts = part_sems.shape[1]
    columns = g_own.shape[1] // parts
    brought = []
    for part in range(parts):
        at = (slice(None), pl.ds(part * columns, columns))
        brought.append(
            [
                pltpu.make_async_copy(source.at[at], target.at[at], part_sems.at[n, part])
                for n, (source, target) in enumerate(
                    (
                        (g_own_hbm, g_own),
                        (g_sib_hbm, g_sib),
                        (u_own_hbm, u_own),
                        (u_sib_hbm, u_sib),
                    )
                )
            ]
        )
        for copy in brought[-1]:
            copy.start()
    later = [
        pltpu.make_async_copy(source, target, whole_sems.at[n])
        for n, (source, target) in enumerate(((d_own_hbm, d_own_ref), (d_sib_hbm, d_sib_ref)))
    ]
    for copy in later:
        copy.start()
    half = g_own.shape[0]
    chips = out_ref.shape[0]
    stream = res_ref[...].astype(f32) + ((p0[...] + p1[...]) + (p2[...] + p3[...]))
    stream_ref[...] = stream
    scaled = stream * gain_ref[0:1, :].astype(f32)
    mine = jnp.where(core == 0, scaled[:, :half], scaled[:, half:]).astype(bf16)
    other = jnp.where(core == 0, scaled[:, half:], scaled[:, :half]).astype(bf16)
    square = jnp.sum(stream * stream, axis=1, keepdims=True)
    square_hi = square.astype(bf16).astype(f32)
    tokens = square.shape[0]
    lane = lax.broadcasted_iota(jnp.int32, (tokens, HD), 1)
    notes = jnp.where(
        lane == 0, square_hi, jnp.where(lane == 1, square - square_hi, 0.0)
    ).astype(bf16)
    notes = jnp.concatenate([notes, jnp.zeros((HD - tokens, HD), bf16)], axis=0)
    unit = (
        lax.broadcasted_iota(jnp.int32, (16, HD), 0) == lax.broadcasted_iota(jnp.int32, (16, HD), 1)
    ).astype(bf16)
    squares = dot(unit, notes, 1, 1).astype(bf16)
    wide = g_own.shape[1] // chips

    def store(k, gate, up):
        for part in range(2):
            at = slice(part * HD, (part + 1) * HD)
            out_ref[k, part * tokens : (part + 1) * tokens, :] = gate[:, at]
            out_ref[k, (2 + part) * tokens : (3 + part) * tokens, :] = up[:, at]
        out_ref[k, 4 * tokens :, :] = squares

    ready = None
    for k in range(chips):
        if k % (chips // parts) == 0:
            for copy in brought[k // (chips // parts)]:
                copy.wait()
        at = slice(k * wide, (k + 1) * wide)
        gate = dot(mine, g_own[:, at]) + dot(other, g_sib[:, at])
        up = dot(mine, u_own[:, at]) + dot(other, u_sib[:, at])
        if ready:
            store(*ready)
        ready = k, gate.astype(bf16), up.astype(bf16)
    store(*ready)
    for copy in later:
        copy.wait()


def down_kernel(where_ref, got_ref, own_ref, sib_ref, out_ref):
    core = where_ref[1]
    chips, tokens, width = out_ref.shape
    total = got_ref[0].astype(f32)
    for i in range(1, chips):
        total = total + got_ref[i].astype(f32)
    square = total[4 * tokens : 4 * tokens + 1, :] + total[4 * tokens + 1 : 4 * tokens + 2, :]
    scale_row = lax.rsqrt(square / D + norm_eps)
    row = lax.broadcasted_iota(jnp.int32, (tokens, HD), 0)
    col = lax.broadcasted_iota(jnp.int32, (tokens, HD), 1)
    scale = jnp.sum(jnp.where(row == col, scale_row, 0.0), axis=1, keepdims=True)
    halves = []
    for part in range(2):
        gate = total[part * tokens : (part + 1) * tokens] * scale
        up = total[(2 + part) * tokens : (3 + part) * tokens] * scale
        halves.append(gate / (1.0 + jnp.exp(-gate)) * up)
    mine = jnp.where(core == 0, halves[0], halves[1]).astype(bf16)
    other = jnp.where(core == 0, halves[1], halves[0]).astype(bf16)
    rows = jnp.concatenate([mine, other], axis=1)
    for k in range(chips):
        at = slice(k * width, (k + 1) * width)
        out_ref[k] = dot(rows, jnp.concatenate([own_ref[:, at], sib_ref[:, at]], axis=0)).astype(bf16)


def on_device(
    keys_cache,
    values_cache,
    keep_blocks,
    keep_count,
    queries,
    new_keys,
    new_values,
    residual_in,
    norm_gain,
    w_out,
    w_gate,
    w_up,
    w_down,
):
    holders = lax.axis_size("seq")
    chips = holders // 2
    holder = lax.axis_index("seq").astype(jnp.int32)
    core = holder % 2
    prompts, positions = keys_cache.shape[:2]
    per_dev = positions // BLK
    list_length = keep_blocks.shape[2]
    tokens = STEPS * chips
    width = residual_in.shape[2]
    where = jnp.stack([holder, core])
    smem = pl.BlockSpec(memory_space=pltpu.SMEM)
    vmem = pl.BlockSpec(memory_space=pltpu.VMEM)
    hbm = pl.BlockSpec(memory_space=pltpu.HBM)
    params = pltpu.CompilerParams(vmem_limit_bytes=24 * MIB)

    same_core = [[2 * i + c for i in range(chips)] for c in range(2)]
    swap = [(i, i ^ 1) for i in range(holders)]

    def over_chips(x):
        return lax.all_to_all(
            x, "seq", split_axis=0, concat_axis=0, tiled=True, axis_index_groups=same_core
        )

    def sibling(x):
        return lax.ppermute(x, "seq", swap)

    def heads(x):
        return [x] + [lax.ppermute(x, "head", [(i, i ^ s) for i in range(4)]) for s in (1, 2, 3)]

    def parity(x, which):
        x = x.reshape(STEPS, chips, 2, width)
        return lax.dynamic_slice_in_dim(x, which, 1, 2).reshape(tokens, width)

    def in_order(own, sib):
        low = jnp.where(core == 0, own, sib)
        high = jnp.where(core == 0, sib, own)
        return jnp.concatenate([low, high], axis=1)

    q_rows = queries.reshape(ROWS, HD)

    half = CAP * BLK
    tile = (chips, 2 * half, KV * HD)
    groups = 4
    dma = pltpu.SemaphoreType.DMA
    to_sib, q_copies, codes = pl.pallas_call(
        gather_kernel,
        in_specs=[smem, smem, vmem, vmem, hbm, hbm],
        out_specs=[hbm, hbm, smem],
        out_shape=[
            jax.ShapeDtypeStruct(tile, bf16),
            jax.ShapeDtypeStruct((chips, ROWS, HD), bf16),
            jax.ShapeDtypeStruct((chips * KV,), jnp.int32),
        ],
        scratch_shapes=[
            pltpu.VMEM((1, list_length), jnp.int32),
            pltpu.SMEM((1, list_length), jnp.int32),
            pltpu.VMEM(tile, bf16),
            dma,
            dma((chips,)),
            dma((groups,)),
            dma((groups,)),
        ],
        compiler_params=pltpu.CompilerParams(vmem_limit_bytes=50 * MIB),
        name="gather",
    )(where, keep_count.T, keep_blocks, q_rows, keys_cache, values_cache)
    q_own = over_chips(q_copies)
    sib_packed = sibling(to_sib)
    partial = pl.pallas_call(
        attend_kernel,
        in_specs=[smem, smem, vmem, hbm, hbm, pl.BlockSpec(memory_space=pl.ANY)],
        out_specs=vmem,
        out_shape=jax.ShapeDtypeStruct((chips, PACK, HD), bf16),
        scratch_shapes=[pltpu.VMEM(tile, bf16)] * 2 + [dma((groups,))] * 2,
        compiler_params=pltpu.CompilerParams(vmem_limit_bytes=50 * MIB),
        name="attend",
    )(where, codes, q_own, keys_cache, values_cache, sib_packed)

    w_out_s, w_gate_s, w_up_s, w_down_s = w_out, w_gate, w_up, w_down
    res_s, gain_s = parity(residual_in, 1 - core), norm_gain
    w_out_sib = sibling(w_out_s)
    w_gate_sib = sibling(w_gate_s)
    w_up_sib = sibling(w_up_s)
    w_down_sib = sibling(w_down_s)
    extra = sibling(jnp.concatenate([res_s, jnp.broadcast_to(gain_s[None], (16, width))], axis=0))
    res = in_order(parity(residual_in, core), extra[:tokens])
    gain = in_order(jnp.broadcast_to(norm_gain[None], (16, width)), extra[tokens:])

    got = over_chips(partial)
    pad = ((0, 16 - STEPS), (0, 0))
    attended = pl.pallas_call(
        combine_kernel,
        in_specs=[vmem] * 4,
        out_specs=vmem,
        out_shape=jax.ShapeDtypeStruct((ROWS, HD), bf16),
        compiler_params=params,
        name="combine",
    )(
        got,
        q_rows,
        jnp.pad(new_keys.reshape(STEPS, KV * HD), pad),
        jnp.pad(new_values.reshape(STEPS, KV * HD), pad),
    )

    all_attended = over_chips(jnp.broadcast_to(attended[None], (chips, ROWS, HD)))
    projected = pl.pallas_call(
        project_kernel,
        in_specs=[smem, vmem, vmem, vmem],
        out_specs=vmem,
        out_shape=jax.ShapeDtypeStruct((tokens, 2 * width), f32),
        scratch_shapes=[pltpu.VMEM((chips * ROWS, HD), f32)],
        compiler_params=params,
        name="project",
    )(where, all_attended, w_out, w_out_sib)
    parts = heads(projected)

    shares, stream, w_down_own, w_down_sib = pl.pallas_call(
        gate_up_kernel,
        in_specs=[smem] + [vmem] * 6 + [hbm] * 6,
        out_specs=[vmem] * 4,
        out_shape=[
            jax.ShapeDtypeStruct((chips, 4 * tokens + 16, HD), bf16),
            jax.ShapeDtypeStruct((tokens, 2 * width), f32),
            jax.ShapeDtypeStruct(w_down.shape, bf16),
            jax.ShapeDtypeStruct(w_down.shape, bf16),
        ],
        scratch_shapes=[pltpu.VMEM(w_gate.shape, bf16)] * 4 + [dma((4, 4)), dma((2,))],
        compiler_params=params,
        name="gate_up",
    )(where, *parts, res, gain, w_gate, w_up, w_gate_sib, w_up_sib, w_down, w_down_sib)

    got_shares = over_chips(shares)
    down = pl.pallas_call(
        down_kernel,
        in_specs=[smem, vmem, vmem, vmem],
        out_specs=vmem,
        out_shape=jax.ShapeDtypeStruct((chips, tokens, 2 * width), bf16),
        compiler_params=params,
        name="down",
    )(where, got_shares, w_down_own, w_down_sib)

    lowered = jnp.sum(over_chips(down).astype(f32), axis=0)
    l0, l1, l2, l3 = heads(lowered)
    final = (stream + ((l0 + l1) + (l2 + l3))).astype(bf16)
    low, high = final[:, :width], final[:, width:]
    keep = jnp.where(core == 0, low, high)
    come = sibling(jnp.where(core == 0, high, low))
    even = jnp.where(core == 0, keep, come).reshape(STEPS, chips, 1, width)
    odd = jnp.where(core == 0, come, keep).reshape(STEPS, chips, 1, width)
    layer_out = jnp.concatenate([even, odd], axis=2).reshape(STEPS, holders, width)
    return (attended.reshape(STEPS, 1, HQ * HD), layer_out)


def solution(mesh):
    placed = (
        P(None, "seq", "head"),
        P(None, "seq", "head"),
        P(None, "head", None),
        P(None, "head"),
        P(None, "seq", "head"),
        P(None, "seq", "head"),
        P(None, "seq", "head"),
        P(None, None, "seq"),
        P("seq"),
        P("head", "seq"),
        P("seq", "head"),
        P("seq", "head"),
        P(("head", "seq"), None),
    )
    return jax.shard_map(
        on_device,
        mesh=mesh,
        in_specs=placed,
        out_specs=(P(None, "seq", "head"), P(None, None, "seq")),
        check_vma=False,
    )
```

```python
import functools

import jax
import jax.numpy as jnp
from jax import lax
from jax.experimental import pallas as pl
from jax.experimental.pallas import tpu as pltpu
from jax.sharding import PartitionSpec as P

D = 8192
H = 64
KVH = 8
HD = 128
BLK = 64
CAP = 4
GROUPS = H // KVH

masked_score = -1e30
norm_eps = 1e-06
score_scale = HD ** (-0.5)

f32 = jnp.float32
bf16 = jnp.bfloat16
MIB = 1 << 20

STEPS = 3
KV = 2
HQ = KV * GROUPS
ROWS = STEPS * HQ
PACK = ROWS + 16


def dot(a, b, ca=1, cb=0):
    return lax.dot_general(a, b, (((ca,), (cb,)), ((), ())), preferred_element_type=f32)


def first_head_rows():
    rows = lax.broadcasted_iota(jnp.int32, (ROWS, 1), 0)
    return (rows // GROUPS) % KV == 0


def two_head_queries(q, first):
    zero = jnp.zeros_like(q)
    return jnp.concatenate([jnp.where(first, q, zero), jnp.where(first, zero, q)], axis=1)


def per_head(values, first):
    return jnp.where(first, values[:, :HD], values[:, HD:])


def pack_prompt(prompt, codes, k_ref, v_ref, packed_ref, sem):
    half = CAP * BLK
    for h in range(KV):
        lanes = pl.ds(h * HD, HD)
        for s in range(CAP):
            at = pl.multiple_of(((codes[h] >> (3 * s)) & 7) * BLK, BLK)
            for part, cache_ref in enumerate((k_ref, v_ref)):
                pltpu.make_async_copy(
                    cache_ref.at[prompt, pl.ds(at, BLK), lanes],
                    packed_ref.at[pl.ds(part * half + s * BLK, BLK), lanes],
                    sem,
                ).start()


def gather_kernel(
    where_ref, count_ref, lists_ref, q_ref, k_ref, v_ref, out_ref, q_out, codes_ref,
    wide_ref, scalar_ref, packed_ref, list_sem, q_sems, in_sems, out_sems,
):
    spread = [
        pltpu.make_async_copy(q_ref, q_out.at[i], q_sems.at[i]) for i in range(q_out.shape[0])
    ]
    for copy in spread:
        copy.start()
    core = where_ref[1]
    per_dev = k_ref.shape[1] // BLK
    base = where_ref[0] * per_dev
    sib_base = (where_ref[0] + 1 - 2 * core) * per_dev
    lists = lists_ref[...]
    lane = lax.broadcasted_iota(jnp.int32, lists.shape, 2)
    valid = (lists > 0) | (lane == 0)
    before = jnp.sum(jnp.where(valid & (lists < base), 1.0, 0.0), axis=2, keepdims=True)
    local = lists - base
    mine = valid & (local >= 0) & (local < per_dev)
    theirs = valid & (lists >= sib_base) & (lists < sib_base + per_dev)
    rank = jnp.clip(lane - before.astype(jnp.int32), 0, CAP - 1)
    share = jnp.where(mine, jnp.left_shift(local, 3 * rank) + (1 << 12), 0)
    share = share + jnp.where(theirs, 1 << 15, 0)
    code = jnp.sum(share.astype(f32), axis=2, keepdims=True).astype(jnp.int32)
    spot = lax.broadcasted_iota(jnp.int32, lists.shape, 0) * KV + lax.broadcasted_iota(
        jnp.int32, lists.shape, 1
    )
    wide_ref[...] = jnp.sum(jnp.sum(jnp.where(lane == spot, code, 0), axis=0), axis=0, keepdims=True)
    listed = pltpu.make_async_copy(wide_ref, scalar_ref, list_sem)
    listed.start()
    listed.wait()

    def code_of(prompt, h):
        return jnp.where(count_ref[h, prompt] > 0, scalar_ref[0, prompt * KV + h], 0)

    chips = packed_ref.shape[0]
    groups = in_sems.shape[0]
    size = chips // groups
    for g in range(groups):

        def one(i, carry):
            chip = g * size + i
            prompt = chip * 2 + 1 - core
            codes = [code_of(prompt, h) for h in range(KV)]
            pack_prompt(prompt, codes, k_ref, v_ref, packed_ref.at[chip], in_sems.at[g])
            for h in range(KV):
                codes_ref[chip * KV + h] = code_of(chip * 2 + core, h)
            return carry

        lax.fori_loop(0, size, one, 0)
    leaving = []
    for g in range(groups):
        at = pl.ds(g * size, size)
        pltpu.make_async_copy(packed_ref.at[at], packed_ref.at[at], in_sems.at[g]).wait()
        leaving.append(pltpu.make_async_copy(packed_ref.at[at], out_ref.at[at], out_sems.at[g]))
        leaving[-1].start()
    for copy in leaving + spread:
        copy.wait()


def attend_kernel(
    where_ref, codes_ref, q_ref, k_ref, v_ref, sib_hbm, out_ref, own_ref, sib_ref, own_sems, sib_sems
):
    core = where_ref[1]
    half = CAP * BLK
    chips = q_ref.shape[0]
    groups = own_sems.shape[0]
    size = chips // groups
    first = first_head_rows()
    lane = lax.broadcasted_iota(jnp.int32, (ROWS, HD), 1)
    slot_lane = lax.broadcasted_iota(jnp.int32, (ROWS, half), 1)
    unit = (
        lax.broadcasted_iota(jnp.int32, (16, HD), 0) == lax.broadcasted_iota(jnp.int32, (16, HD), 1)
    ).astype(bf16)

    def from_sib(g):
        at = pl.ds(g * size, size)
        return pltpu.make_async_copy(sib_hbm.at[at], sib_ref.at[at], sib_sems.at[g])

    def fetch(g):
        from_sib(g).start()

        def one(i, carry):
            chip = g * size + i
            codes = [codes_ref[chip * KV + h] for h in range(KV)]
            pack_prompt(chip * 2 + core, codes, k_ref, v_ref, own_ref.at[chip], own_sems.at[g])
            return carry

        lax.fori_loop(0, size, one, 0)

    def score_of(chip):
        queries = two_head_queries(q_ref[chip], first)
        scores, keeps = [], []
        for shift, blocks_ref in ((12, own_ref), (15, sib_ref)):
            ends = [((codes_ref[chip * KV + h] >> shift) & 7) * BLK for h in range(KV)]
            keeps.append(slot_lane < jnp.where(first, ends[0], ends[1]))
            scores.append(dot(queries, blocks_ref[chip, :half, :], 1, 1))
        return jnp.concatenate(keeps, axis=1), jnp.concatenate(scores, axis=1)

    def weigh(keep, score):
        score = jnp.where(keep, score * score_scale, masked_score)
        top = jnp.max(score, axis=1, keepdims=True).astype(bf16).astype(f32)
        weight = jnp.where(keep, jnp.exp(score - top), 0.0).astype(bf16)
        return top, weight, jnp.sum(weight.astype(f32), axis=1, keepdims=True)

    def store(chip, top, weight, total):
        summed = per_head(
            dot(weight[:, :half], own_ref[chip, half:, :])
            + dot(weight[:, half:], sib_ref[chip, half:, :]),
            first,
        )
        total_hi = total.astype(bf16).astype(f32)
        notes = jnp.where(
            lane == 0, top, jnp.where(lane == 1, total_hi, jnp.where(lane == 2, total - total_hi, 0.0))
        ).astype(bf16)
        notes = jnp.concatenate([notes, jnp.zeros((HD - ROWS, HD), bf16)], axis=0)
        out_ref[chip, :ROWS, :] = summed.astype(bf16)
        out_ref[chip, ROWS:, :] = dot(unit, notes, 1, 1).astype(bf16)

    for g in range(groups):
        fetch(g)
    for g in range(groups):
        at = pl.ds(g * size, size)
        pltpu.make_async_copy(own_ref.at[at], own_ref.at[at], own_sems.at[g]).wait()
        from_sib(g).wait()
        chips_now = range(g * size, (g + 1) * size)
        scored = [score_of(chip) for chip in chips_now]
        weighed = [weigh(*each) for each in scored]
        for chip, each in zip(chips_now, weighed):
            store(chip, *each)


def combine_kernel(got_ref, q_ref, nk_ref, nv_ref, out_ref):
    holders = got_ref.shape[0]
    notes = got_ref[:, ROWS:, :].reshape(holders * 16, HD)
    row = lax.broadcasted_iota(jnp.int32, (holders * 16, HD), 0)
    col = lax.broadcasted_iota(jnp.int32, (holders * 16, HD), 1)
    pick = ((col == (row % 16) * holders + row // 16) & (row % 16 < 3)).astype(bf16)
    columns = dot(notes, pick, 0, 0)[:ROWS]
    tops = columns[:, :holders]
    totals = columns[:, holders : 2 * holders] + columns[:, 2 * holders : 3 * holders]
    first = first_head_rows()
    new_score = dot(two_head_queries(q_ref[...], first), nk_ref[...], 1, 1) * score_scale
    step = lax.broadcasted_iota(jnp.int32, new_score.shape, 0) // HQ
    token = lax.broadcasted_iota(jnp.int32, new_score.shape, 1)
    causal = token <= step
    new_score = jnp.where(causal, new_score, masked_score)
    top = jnp.maximum(
        jnp.max(tops, axis=1, keepdims=True), jnp.max(new_score, axis=1, keepdims=True)
    )
    share = jnp.exp(tops - top)
    new_weight = jnp.where(causal, jnp.exp(new_score - top), 0.0).astype(bf16)
    total = jnp.sum(share * totals, axis=1, keepdims=True) + jnp.sum(
        new_weight.astype(f32), axis=1, keepdims=True
    )
    summed = per_head(dot(new_weight, nv_ref[...]), first)
    for i in range(holders):
        summed = summed + share[:, i : i + 1] * got_ref[i, :ROWS, :].astype(f32)
    out_ref[...] = (summed / total).astype(bf16)


def project_kernel(where_ref, got_ref, own_ref, sib_ref, out_ref, wide_ref):
    core = where_ref[1]
    chips = got_ref.shape[0]
    wide_ref[...] = got_ref[...].reshape(chips * ROWS, HD).astype(f32)
    own = jnp.zeros((STEPS * chips, own_ref.shape[1]), f32)
    sib = jnp.zeros((STEPS * chips, own_ref.shape[1]), f32)
    for pair in range(HQ // 2):
        parts = []
        for h in (2 * pair, 2 * pair + 1):
            parts.append(
                jnp.concatenate(
                    [wide_ref[pl.ds(t * HQ + h, chips, stride=ROWS), :] for t in range(STEPS)], axis=0
                )
            )
        rows = jnp.concatenate(parts, axis=1).astype(bf16)
        at = slice(pair * 2 * HD, (pair + 1) * 2 * HD)
        own = own + dot(rows, own_ref[at, :])
        sib = sib + dot(rows, sib_ref[at, :])
    half = own_ref.shape[1]
    out_ref[:, :half] = jnp.where(core == 0, own, sib)
    out_ref[:, half:] = jnp.where(core == 0, sib, own)


def gate_up_kernel(
    where_ref, p0, p1, p2, p3, res_ref, gain_ref, g_own_hbm, u_own_hbm, g_sib_hbm, u_sib_hbm,
    d_own_hbm, d_sib_hbm, out_ref, stream_ref, d_own_ref, d_sib_ref, g_own, u_own, g_sib, u_sib,
    part_sems, whole_sems,
):
    core = where_ref[1]
    parts = part_sems.shape[1]
    columns = g_own.shape[1] // parts
    brought = []
    for part in range(parts):
        at = (slice(None), pl.ds(part * columns, columns))
        brought.append(
            [
                pltpu.make_async_copy(source.at[at], target.at[at], part_sems.at[n, part])
                for n, (source, target) in enumerate(
                    (
                        (g_own_hbm, g_own),
                        (g_sib_hbm, g_sib),
                        (u_own_hbm, u_own),
                        (u_sib_hbm, u_sib),
                    )
                )
            ]
        )
        for copy in brought[-1]:
            copy.start()
    later = [
        pltpu.make_async_copy(source, target, whole_sems.at[n])
        for n, (source, target) in enumerate(((d_own_hbm, d_own_ref), (d_sib_hbm, d_sib_ref)))
    ]
    for copy in later:
        copy.start()
    half = g_own.shape[0]
    chips = out_ref.shape[0]
    stream = res_ref[...].astype(f32) + ((p0[...] + p1[...]) + (p2[...] + p3[...]))
    stream_ref[...] = stream
    scaled = stream * gain_ref[0:1, :].astype(f32)
    mine = jnp.where(core == 0, scaled[:, :half], scaled[:, half:]).astype(bf16)
    other = jnp.where(core == 0, scaled[:, half:], scaled[:, :half]).astype(bf16)
    square = jnp.sum(stream * stream, axis=1, keepdims=True)
    square_hi = square.astype(bf16).astype(f32)
    tokens = square.shape[0]
    lane = lax.broadcasted_iota(jnp.int32, (tokens, HD), 1)
    notes = jnp.where(
        lane == 0, square_hi, jnp.where(lane == 1, square - square_hi, 0.0)
    ).astype(bf16)
    notes = jnp.concatenate([notes, jnp.zeros((HD - tokens, HD), bf16)], axis=0)
    unit = (
        lax.broadcasted_iota(jnp.int32, (16, HD), 0) == lax.broadcasted_iota(jnp.int32, (16, HD), 1)
    ).astype(bf16)
    squares = dot(unit, notes, 1, 1).astype(bf16)
    wide = g_own.shape[1] // chips

    def store(k, gate, up):
        for part in range(2):
            at = slice(part * HD, (part + 1) * HD)
            out_ref[k, part * tokens : (part + 1) * tokens, :] = gate[:, at]
            out_ref[k, (2 + part) * tokens : (3 + part) * tokens, :] = up[:, at]
        out_ref[k, 4 * tokens :, :] = squares

    ready = None
    for k in range(chips):
        if k % (chips // parts) == 0:
            for copy in brought[k // (chips // parts)]:
                copy.wait()
        at = slice(k * wide, (k + 1) * wide)
        gate = dot(mine, g_own[:, at]) + dot(other, g_sib[:, at])
        up = dot(mine, u_own[:, at]) + dot(other, u_sib[:, at])
        if ready:
            store(*ready)
        ready = k, gate.astype(bf16), up.astype(bf16)
    store(*ready)
    for copy in later:
        copy.wait()


def down_kernel(where_ref, got_ref, own_ref, sib_ref, out_ref):
    core = where_ref[1]
    chips, tokens, width = out_ref.shape
    total = got_ref[0].astype(f32)
    for i in range(1, chips):
        total = total + got_ref[i].astype(f32)
    square = total[4 * tokens : 4 * tokens + 1, :] + total[4 * tokens + 1 : 4 * tokens + 2, :]
    scale_row = lax.rsqrt(square / D + norm_eps)
    row = lax.broadcasted_iota(jnp.int32, (tokens, HD), 0)
    col = lax.broadcasted_iota(jnp.int32, (tokens, HD), 1)
    scale = jnp.sum(jnp.where(row == col, scale_row, 0.0), axis=1, keepdims=True)
    halves = []
    for part in range(2):
        gate = total[part * tokens : (part + 1) * tokens] * scale
        up = total[(2 + part) * tokens : (3 + part) * tokens] * scale
        halves.append(gate / (1.0 + jnp.exp(-gate)) * up)
    mine = jnp.where(core == 0, halves[0], halves[1]).astype(bf16)
    other = jnp.where(core == 0, halves[1], halves[0]).astype(bf16)
    rows = jnp.concatenate([mine, other], axis=1)
    for k in range(chips):
        at = slice(k * width, (k + 1) * width)
        out_ref[k] = dot(rows, jnp.concatenate([own_ref[:, at], sib_ref[:, at]], axis=0)).astype(bf16)


def on_device(
    keys_cache,
    values_cache,
    keep_blocks,
    keep_count,
    queries,
    new_keys,
    new_values,
    residual_in,
    norm_gain,
    w_out,
    w_gate,
    w_up,
    w_down,
):
    holders = lax.axis_size("seq")
    chips = holders // 2
    holder = lax.axis_index("seq").astype(jnp.int32)
    core = holder % 2
    prompts, positions = keys_cache.shape[:2]
    per_dev = positions // BLK
    list_length = keep_blocks.shape[2]
    tokens = STEPS * chips
    width = residual_in.shape[2]
    where = jnp.stack([holder, core])
    smem = pl.BlockSpec(memory_space=pltpu.SMEM)
    vmem = pl.BlockSpec(memory_space=pltpu.VMEM)
    hbm = pl.BlockSpec(memory_space=pltpu.HBM)
    params = pltpu.CompilerParams(vmem_limit_bytes=24 * MIB)

    same_core = [[2 * i + c for i in range(chips)] for c in range(2)]
    swap = [(i, i ^ 1) for i in range(holders)]

    def over_chips(x):
        return lax.all_to_all(
            x, "seq", split_axis=0, concat_axis=0, tiled=True, axis_index_groups=same_core
        )

    def sibling(x):
        return lax.ppermute(x, "seq", swap)

    def heads(x):
        return [x] + [lax.ppermute(x, "head", [(i, i ^ s) for i in range(4)]) for s in (1, 2, 3)]

    def parity(x, which):
        x = x.reshape(STEPS, chips, 2, width)
        return lax.dynamic_slice_in_dim(x, which, 1, 2).reshape(tokens, width)

    def in_order(own, sib):
        low = jnp.where(core == 0, own, sib)
        high = jnp.where(core == 0, sib, own)
        return jnp.concatenate([low, high], axis=1)

    q_rows = queries.reshape(ROWS, HD)

    half = CAP * BLK
    tile = (chips, 2 * half, KV * HD)
    groups = 4
    dma = pltpu.SemaphoreType.DMA
    to_sib, q_copies, codes = pl.pallas_call(
        gather_kernel,
        in_specs=[smem, smem, vmem, vmem, hbm, hbm],
        out_specs=[hbm, hbm, smem],
        out_shape=[
            jax.ShapeDtypeStruct(tile, bf16),
            jax.ShapeDtypeStruct((chips, ROWS, HD), bf16),
            jax.ShapeDtypeStruct((chips * KV,), jnp.int32),
        ],
        scratch_shapes=[
            pltpu.VMEM((1, list_length), jnp.int32),
            pltpu.SMEM((1, list_length), jnp.int32),
            pltpu.VMEM(tile, bf16),
            dma,
            dma((chips,)),
            dma((groups,)),
            dma((groups,)),
        ],
        compiler_params=pltpu.CompilerParams(vmem_limit_bytes=50 * MIB),
        name="gather",
    )(where, keep_count.T, keep_blocks, q_rows, keys_cache, values_cache)
    q_own = over_chips(q_copies)
    sib_packed = sibling(to_sib)
    partial = pl.pallas_call(
        attend_kernel,
        in_specs=[smem, smem, vmem, hbm, hbm, pl.BlockSpec(memory_space=pl.ANY)],
        out_specs=vmem,
        out_shape=jax.ShapeDtypeStruct((chips, PACK, HD), bf16),
        scratch_shapes=[pltpu.VMEM(tile, bf16)] * 2 + [dma((groups,))] * 2,
        compiler_params=pltpu.CompilerParams(vmem_limit_bytes=50 * MIB),
        name="attend",
    )(where, codes, q_own, keys_cache, values_cache, sib_packed)

    w_out_s, w_gate_s, w_up_s, w_down_s = w_out, w_gate, w_up, w_down
    res_s, gain_s = parity(residual_in, 1 - core), norm_gain
    w_out_sib = sibling(w_out_s)
    w_gate_sib = sibling(w_gate_s)
    w_up_sib = sibling(w_up_s)
    w_down_sib = sibling(w_down_s)
    extra = sibling(jnp.concatenate([res_s, jnp.broadcast_to(gain_s[None], (16, width))], axis=0))
    res = in_order(parity(residual_in, core), extra[:tokens])
    gain = in_order(jnp.broadcast_to(norm_gain[None], (16, width)), extra[tokens:])

    got = over_chips(partial)
    pad = ((0, 16 - STEPS), (0, 0))
    attended = pl.pallas_call(
        combine_kernel,
        in_specs=[vmem] * 4,
        out_specs=vmem,
        out_shape=jax.ShapeDtypeStruct((ROWS, HD), bf16),
        compiler_params=params,
        name="combine",
    )(
        got,
        q_rows,
        jnp.pad(new_keys.reshape(STEPS, KV * HD), pad),
        jnp.pad(new_values.reshape(STEPS, KV * HD), pad),
    )

    all_attended = over_chips(jnp.broadcast_to(attended[None], (chips, ROWS, HD)))
    projected = pl.pallas_call(
        project_kernel,
        in_specs=[smem, vmem, vmem, vmem],
        out_specs=vmem,
        out_shape=jax.ShapeDtypeStruct((tokens, 2 * width), f32),
        scratch_shapes=[pltpu.VMEM((chips * ROWS, HD), f32)],
        compiler_params=params,
        name="project",
    )(where, all_attended, w_out, w_out_sib)
    parts = heads(projected)

    shares, stream, w_down_own, w_down_sib = pl.pallas_call(
        gate_up_kernel,
        in_specs=[smem] + [vmem] * 6 + [hbm] * 6,
        out_specs=[vmem] * 4,
        out_shape=[
            jax.ShapeDtypeStruct((chips, 4 * tokens + 16, HD), bf16),
            jax.ShapeDtypeStruct((tokens, 2 * width), f32),
            jax.ShapeDtypeStruct(w_down.shape, bf16),
            jax.ShapeDtypeStruct(w_down.shape, bf16),
        ],
        scratch_shapes=[pltpu.VMEM(w_gate.shape, bf16)] * 4 + [dma((4, 8)), dma((2,))],
        compiler_params=params,
        name="gate_up",
    )(where, *parts, res, gain, w_gate, w_up, w_gate_sib, w_up_sib, w_down, w_down_sib)

    got_shares = over_chips(shares)
    down = pl.pallas_call(
        down_kernel,
        in_specs=[smem, vmem, vmem, vmem],
        out_specs=vmem,
        out_shape=jax.ShapeDtypeStruct((chips, tokens, 2 * width), bf16),
        compiler_params=params,
        name="down",
    )(where, got_shares, w_down_own, w_down_sib)

    lowered = jnp.sum(over_chips(down).astype(f32), axis=0)
    l0, l1, l2, l3 = heads(lowered)
    final = (stream + ((l0 + l1) + (l2 + l3))).astype(bf16)
    low, high = final[:, :width], final[:, width:]
    keep = jnp.where(core == 0, low, high)
    come = sibling(jnp.where(core == 0, high, low))
    even = jnp.where(core == 0, keep, come).reshape(STEPS, chips, 1, width)
    odd = jnp.where(core == 0, come, keep).reshape(STEPS, chips, 1, width)
    layer_out = jnp.concatenate([even, odd], axis=2).reshape(STEPS, holders, width)
    return (attended.reshape(STEPS, 1, HQ * HD), layer_out)


def solution(mesh):
    placed = (
        P(None, "seq", "head"),
        P(None, "seq", "head"),
        P(None, "head", None),
        P(None, "head"),
        P(None, "seq", "head"),
        P(None, "seq", "head"),
        P(None, "seq", "head"),
        P(None, None, "seq"),
        P("seq"),
        P("head", "seq"),
        P("seq", "head"),
        P("seq", "head"),
        P(("head", "seq"), None),
    )
    return jax.shard_map(
        on_device,
        mesh=mesh,
        in_specs=placed,
        out_specs=(P(None, "seq", "head"), P(None, None, "seq")),
        check_vma=False,
    )
```

```python
import functools

import jax
import jax.numpy as jnp
from jax import lax
from jax.experimental import pallas as pl
from jax.experimental.pallas import tpu as pltpu
from jax.sharding import PartitionSpec as P

D = 8192
H = 64
KVH = 8
HD = 128
BLK = 64
CAP = 4
GROUPS = H // KVH

masked_score = -1e30
norm_eps = 1e-06
score_scale = HD ** (-0.5)

f32 = jnp.float32
bf16 = jnp.bfloat16
MIB = 1 << 20

STEPS = 3
KV = 2
HQ = KV * GROUPS
ROWS = STEPS * HQ
PACK = ROWS + 16


def dot(a, b, ca=1, cb=0):
    return lax.dot_general(a, b, (((ca,), (cb,)), ((), ())), preferred_element_type=f32)


def first_head_rows():
    rows = lax.broadcasted_iota(jnp.int32, (ROWS, 1), 0)
    return (rows // GROUPS) % KV == 0


def two_head_queries(q, first):
    zero = jnp.zeros_like(q)
    return jnp.concatenate([jnp.where(first, q, zero), jnp.where(first, zero, q)], axis=1)


def per_head(values, first):
    return jnp.where(first, values[:, :HD], values[:, HD:])


def pack_prompt(prompt, codes, k_ref, v_ref, packed_ref, sem):
    half = CAP * BLK
    for h in range(KV):
        lanes = pl.ds(h * HD, HD)
        for s in range(CAP):
            at = pl.multiple_of(((codes[h] >> (3 * s)) & 7) * BLK, BLK)
            for part, cache_ref in enumerate((k_ref, v_ref)):
                pltpu.make_async_copy(
                    cache_ref.at[prompt, pl.ds(at, BLK), lanes],
                    packed_ref.at[pl.ds(part * half + s * BLK, BLK), lanes],
                    sem,
                ).start()


def gather_kernel(
    where_ref, count_ref, lists_ref, q_ref, k_ref, v_ref, out_ref, q_out, codes_ref,
    wide_ref, scalar_ref, packed_ref, list_sem, q_sems, in_sems, out_sems,
):
    spread = [
        pltpu.make_async_copy(q_ref, q_out.at[i], q_sems.at[i]) for i in range(q_out.shape[0])
    ]
    for copy in spread:
        copy.start()
    core = where_ref[1]
    per_dev = k_ref.shape[1] // BLK
    base = where_ref[0] * per_dev
    sib_base = (where_ref[0] + 1 - 2 * core) * per_dev
    lists = lists_ref[...]
    lane = lax.broadcasted_iota(jnp.int32, lists.shape, 2)
    valid = (lists > 0) | (lane == 0)
    before = jnp.sum(jnp.where(valid & (lists < base), 1.0, 0.0), axis=2, keepdims=True)
    local = lists - base
    mine = valid & (local >= 0) & (local < per_dev)
    theirs = valid & (lists >= sib_base) & (lists < sib_base + per_dev)
    rank = jnp.clip(lane - before.astype(jnp.int32), 0, CAP - 1)
    share = jnp.where(mine, jnp.left_shift(local, 3 * rank) + (1 << 12), 0)
    share = share + jnp.where(theirs, 1 << 15, 0)
    code = jnp.sum(share.astype(f32), axis=2, keepdims=True).astype(jnp.int32)
    spot = lax.broadcasted_iota(jnp.int32, lists.shape, 0) * KV + lax.broadcasted_iota(
        jnp.int32, lists.shape, 1
    )
    wide_ref[...] = jnp.sum(jnp.sum(jnp.where(lane == spot, code, 0), axis=0), axis=0, keepdims=True)
    listed = pltpu.make_async_copy(wide_ref, scalar_ref, list_sem)
    listed.start()
    listed.wait()

    def code_of(prompt, h):
        return jnp.where(count_ref[h, prompt] > 0, scalar_ref[0, prompt * KV + h], 0)

    chips = packed_ref.shape[0]
    groups = in_sems.shape[0]
    size = chips // groups
    for g in range(groups):

        def one(i, carry):
            chip = g * size + i
            prompt = chip * 2 + 1 - core
            codes = [code_of(prompt, h) for h in range(KV)]
            pack_prompt(prompt, codes, k_ref, v_ref, packed_ref.at[chip], in_sems.at[g])
            for h in range(KV):
                codes_ref[chip * KV + h] = code_of(chip * 2 + core, h)
            return carry

        lax.fori_loop(0, size, one, 0)
    leaving = []
    for g in range(groups):
        at = pl.ds(g * size, size)
        pltpu.make_async_copy(packed_ref.at[at], packed_ref.at[at], in_sems.at[g]).wait()
        leaving.append(pltpu.make_async_copy(packed_ref.at[at], out_ref.at[at], out_sems.at[g]))
        leaving[-1].start()
    for copy in leaving + spread:
        copy.wait()


def attend_kernel(
    where_ref, codes_ref, q_ref, k_ref, v_ref, sib_hbm, out_ref, own_ref, sib_ref, own_sems, sib_sems
):
    core = where_ref[1]
    half = CAP * BLK
    chips = q_ref.shape[0]
    groups = own_sems.shape[0]
    size = chips // groups
    first = first_head_rows()
    lane = lax.broadcasted_iota(jnp.int32, (ROWS, HD), 1)
    slot_lane = lax.broadcasted_iota(jnp.int32, (ROWS, half), 1)
    unit = (
        lax.broadcasted_iota(jnp.int32, (16, HD), 0) == lax.broadcasted_iota(jnp.int32, (16, HD), 1)
    ).astype(bf16)

    def from_sib(g):
        at = pl.ds(g * size, size)
        return pltpu.make_async_copy(sib_hbm.at[at], sib_ref.at[at], sib_sems.at[g])

    def fetch(g):
        from_sib(g).start()

        def one(i, carry):
            chip = g * size + i
            codes = [codes_ref[chip * KV + h] for h in range(KV)]
            pack_prompt(chip * 2 + core, codes, k_ref, v_ref, own_ref.at[chip], own_sems.at[g])
            return carry

        lax.fori_loop(0, size, one, 0)

    def score_of(chip):
        queries = two_head_queries(q_ref[chip], first)
        scores, keeps = [], []
        for shift, blocks_ref in ((12, own_ref), (15, sib_ref)):
            ends = [((codes_ref[chip * KV + h] >> shift) & 7) * BLK for h in range(KV)]
            keeps.append(slot_lane < jnp.where(first, ends[0], ends[1]))
            scores.append(dot(queries, blocks_ref[chip, :half, :], 1, 1))
        return jnp.concatenate(keeps, axis=1), jnp.concatenate(scores, axis=1)

    def weigh(keep, score):
        score = jnp.where(keep, score * score_scale, masked_score)
        top = jnp.max(score, axis=1, keepdims=True).astype(bf16).astype(f32)
        weight = jnp.where(keep, jnp.exp(score - top), 0.0).astype(bf16)
        return top, weight, jnp.sum(weight.astype(f32), axis=1, keepdims=True)

    def store(chip, top, weight, total):
        summed = per_head(
            dot(weight[:, :half], own_ref[chip, half:, :])
            + dot(weight[:, half:], sib_ref[chip, half:, :]),
            first,
        )
        total_hi = total.astype(bf16).astype(f32)
        notes = jnp.where(
            lane == 0, top, jnp.where(lane == 1, total_hi, jnp.where(lane == 2, total - total_hi, 0.0))
        ).astype(bf16)
        notes = jnp.concatenate([notes, jnp.zeros((HD - ROWS, HD), bf16)], axis=0)
        out_ref[chip, :ROWS, :] = summed.astype(bf16)
        out_ref[chip, ROWS:, :] = dot(unit, notes, 1, 1).astype(bf16)

    for g in range(groups):
        fetch(g)
    for g in range(groups):
        at = pl.ds(g * size, size)
        pltpu.make_async_copy(own_ref.at[at], own_ref.at[at], own_sems.at[g]).wait()
        from_sib(g).wait()
        chips_now = range(g * size, (g + 1) * size)
        scored = [score_of(chip) for chip in chips_now]
        weighed = [weigh(*each) for each in scored]
        for chip, each in zip(chips_now, weighed):
            store(chip, *each)


def combine_kernel(got_ref, q_ref, nk_ref, nv_ref, out_ref):
    holders = got_ref.shape[0]
    notes = got_ref[:, ROWS:, :].reshape(holders * 16, HD)
    row = lax.broadcasted_iota(jnp.int32, (holders * 16, HD), 0)
    col = lax.broadcasted_iota(jnp.int32, (holders * 16, HD), 1)
    pick = ((col == (row % 16) * holders + row // 16) & (row % 16 < 3)).astype(bf16)
    columns = dot(notes, pick, 0, 0)[:ROWS]
    tops = columns[:, :holders]
    totals = columns[:, holders : 2 * holders] + columns[:, 2 * holders : 3 * holders]
    first = first_head_rows()
    new_score = dot(two_head_queries(q_ref[...], first), nk_ref[...], 1, 1) * score_scale
    step = lax.broadcasted_iota(jnp.int32, new_score.shape, 0) // HQ
    token = lax.broadcasted_iota(jnp.int32, new_score.shape, 1)
    causal = token <= step
    new_score = jnp.where(causal, new_score, masked_score)
    top = jnp.maximum(
        jnp.max(tops, axis=1, keepdims=True), jnp.max(new_score, axis=1, keepdims=True)
    )
    share = jnp.exp(tops - top)
    new_weight = jnp.where(causal, jnp.exp(new_score - top), 0.0).astype(bf16)
    total = jnp.sum(share * totals, axis=1, keepdims=True) + jnp.sum(
        new_weight.astype(f32), axis=1, keepdims=True
    )
    summed = per_head(dot(new_weight, nv_ref[...]), first)
    for i in range(holders):
        summed = summed + share[:, i : i + 1] * got_ref[i, :ROWS, :].astype(f32)
    out_ref[...] = (summed / total).astype(bf16)


def project_kernel(where_ref, got_ref, own_ref, sib_ref, out_ref, wide_ref):
    core = where_ref[1]
    chips = got_ref.shape[0]
    wide_ref[...] = got_ref[...].reshape(chips * ROWS, HD).astype(f32)
    own = jnp.zeros((STEPS * chips, own_ref.shape[1]), f32)
    sib = jnp.zeros((STEPS * chips, own_ref.shape[1]), f32)
    for pair in range(HQ // 2):
        parts = []
        for h in (2 * pair, 2 * pair + 1):
            parts.append(
                jnp.concatenate(
                    [wide_ref[pl.ds(t * HQ + h, chips, stride=ROWS), :] for t in range(STEPS)], axis=0
                )
            )
        rows = jnp.concatenate(parts, axis=1).astype(bf16)
        at = slice(pair * 2 * HD, (pair + 1) * 2 * HD)
        own = own + dot(rows, own_ref[at, :])
        sib = sib + dot(rows, sib_ref[at, :])
    half = own_ref.shape[1]
    out_ref[:, :half] = jnp.where(core == 0, own, sib).astype(bf16)
    out_ref[:, half:] = jnp.where(core == 0, sib, own).astype(bf16)


def gate_up_kernel(
    where_ref, p0, p1, p2, p3, res_ref, gain_ref, g_own_hbm, u_own_hbm, g_sib_hbm, u_sib_hbm,
    d_own_hbm, d_sib_hbm, out_ref, stream_ref, d_own_ref, d_sib_ref, g_own, u_own, g_sib, u_sib,
    part_sems, whole_sems,
):
    core = where_ref[1]
    parts = part_sems.shape[1]
    columns = g_own.shape[1] // parts
    brought = []
    for part in range(parts):
        at = (slice(None), pl.ds(part * columns, columns))
        brought.append(
            [
                pltpu.make_async_copy(source.at[at], target.at[at], part_sems.at[n, part])
                for n, (source, target) in enumerate(
                    (
                        (g_own_hbm, g_own),
                        (g_sib_hbm, g_sib),
                        (u_own_hbm, u_own),
                        (u_sib_hbm, u_sib),
                    )
                )
            ]
        )
        for copy in brought[-1]:
            copy.start()
    later = [
        pltpu.make_async_copy(source, target, whole_sems.at[n])
        for n, (source, target) in enumerate(((d_own_hbm, d_own_ref), (d_sib_hbm, d_sib_ref)))
    ]
    for copy in later:
        copy.start()
    half = g_own.shape[0]
    chips = out_ref.shape[0]
    stream = res_ref[...].astype(f32) + (
        (p0[...].astype(f32) + p1[...].astype(f32)) + (p2[...].astype(f32) + p3[...].astype(f32))
    )
    stream_ref[...] = stream
    scaled = stream * gain_ref[0:1, :].astype(f32)
    mine = jnp.where(core == 0, scaled[:, :half], scaled[:, half:]).astype(bf16)
    other = jnp.where(core == 0, scaled[:, half:], scaled[:, :half]).astype(bf16)
    square = jnp.sum(stream * stream, axis=1, keepdims=True)
    square_hi = square.astype(bf16).astype(f32)
    tokens = square.shape[0]
    lane = lax.broadcasted_iota(jnp.int32, (tokens, HD), 1)
    notes = jnp.where(
        lane == 0, square_hi, jnp.where(lane == 1, square - square_hi, 0.0)
    ).astype(bf16)
    notes = jnp.concatenate([notes, jnp.zeros((HD - tokens, HD), bf16)], axis=0)
    unit = (
        lax.broadcasted_iota(jnp.int32, (16, HD), 0) == lax.broadcasted_iota(jnp.int32, (16, HD), 1)
    ).astype(bf16)
    squares = dot(unit, notes, 1, 1).astype(bf16)
    wide = g_own.shape[1] // chips

    def store(k, gate, up):
        for part in range(2):
            at = slice(part * HD, (part + 1) * HD)
            out_ref[k, part * tokens : (part + 1) * tokens, :] = gate[:, at]
            out_ref[k, (2 + part) * tokens : (3 + part) * tokens, :] = up[:, at]
        out_ref[k, 4 * tokens :, :] = squares

    ready = None
    for k in range(chips):
        if k % (chips // parts) == 0:
            for copy in brought[k // (chips // parts)]:
                copy.wait()
        at = slice(k * wide, (k + 1) * wide)
        gate = dot(mine, g_own[:, at]) + dot(other, g_sib[:, at])
        up = dot(mine, u_own[:, at]) + dot(other, u_sib[:, at])
        if ready:
            store(*ready)
        ready = k, gate.astype(bf16), up.astype(bf16)
    store(*ready)
    for copy in later:
        copy.wait()


def down_kernel(where_ref, got_ref, own_ref, sib_ref, out_ref):
    core = where_ref[1]
    chips, tokens, width = out_ref.shape
    total = got_ref[0].astype(f32)
    for i in range(1, chips):
        total = total + got_ref[i].astype(f32)
    square = total[4 * tokens : 4 * tokens + 1, :] + total[4 * tokens + 1 : 4 * tokens + 2, :]
    scale_row = lax.rsqrt(square / D + norm_eps)
    row = lax.broadcasted_iota(jnp.int32, (tokens, HD), 0)
    col = lax.broadcasted_iota(jnp.int32, (tokens, HD), 1)
    scale = jnp.sum(jnp.where(row == col, scale_row, 0.0), axis=1, keepdims=True)
    halves = []
    for part in range(2):
        gate = total[part * tokens : (part + 1) * tokens] * scale
        up = total[(2 + part) * tokens : (3 + part) * tokens] * scale
        halves.append(gate / (1.0 + jnp.exp(-gate)) * up)
    mine = jnp.where(core == 0, halves[0], halves[1]).astype(bf16)
    other = jnp.where(core == 0, halves[1], halves[0]).astype(bf16)
    rows = jnp.concatenate([mine, other], axis=1)
    for k in range(chips):
        at = slice(k * width, (k + 1) * width)
        out_ref[k] = dot(rows, jnp.concatenate([own_ref[:, at], sib_ref[:, at]], axis=0)).astype(bf16)


def on_device(
    keys_cache,
    values_cache,
    keep_blocks,
    keep_count,
    queries,
    new_keys,
    new_values,
    residual_in,
    norm_gain,
    w_out,
    w_gate,
    w_up,
    w_down,
):
    holders = lax.axis_size("seq")
    chips = holders // 2
    holder = lax.axis_index("seq").astype(jnp.int32)
    core = holder % 2
    prompts, positions = keys_cache.shape[:2]
    per_dev = positions // BLK
    list_length = keep_blocks.shape[2]
    tokens = STEPS * chips
    width = residual_in.shape[2]
    where = jnp.stack([holder, core])
    smem = pl.BlockSpec(memory_space=pltpu.SMEM)
    vmem = pl.BlockSpec(memory_space=pltpu.VMEM)
    hbm = pl.BlockSpec(memory_space=pltpu.HBM)
    params = pltpu.CompilerParams(vmem_limit_bytes=24 * MIB)

    same_core = [[2 * i + c for i in range(chips)] for c in range(2)]
    swap = [(i, i ^ 1) for i in range(holders)]

    def over_chips(x):
        return lax.all_to_all(
            x, "seq", split_axis=0, concat_axis=0, tiled=True, axis_index_groups=same_core
        )

    def sibling(x):
        return lax.ppermute(x, "seq", swap)

    def heads(x):
        return [x] + [lax.ppermute(x, "head", [(i, i ^ s) for i in range(4)]) for s in (1, 2, 3)]

    def parity(x, which):
        x = x.reshape(STEPS, chips, 2, width)
        return lax.dynamic_slice_in_dim(x, which, 1, 2).reshape(tokens, width)

    def in_order(own, sib):
        low = jnp.where(core == 0, own, sib)
        high = jnp.where(core == 0, sib, own)
        return jnp.concatenate([low, high], axis=1)

    q_rows = queries.reshape(ROWS, HD)

    half = CAP * BLK
    tile = (chips, 2 * half, KV * HD)
    groups = 4
    dma = pltpu.SemaphoreType.DMA
    to_sib, q_copies, codes = pl.pallas_call(
        gather_kernel,
        in_specs=[smem, smem, vmem, vmem, hbm, hbm],
        out_specs=[hbm, hbm, smem],
        out_shape=[
            jax.ShapeDtypeStruct(tile, bf16),
            jax.ShapeDtypeStruct((chips, ROWS, HD), bf16),
            jax.ShapeDtypeStruct((chips * KV,), jnp.int32),
        ],
        scratch_shapes=[
            pltpu.VMEM((1, list_length), jnp.int32),
            pltpu.SMEM((1, list_length), jnp.int32),
            pltpu.VMEM(tile, bf16),
            dma,
            dma((chips,)),
            dma((groups,)),
            dma((groups,)),
        ],
        compiler_params=pltpu.CompilerParams(vmem_limit_bytes=50 * MIB),
        name="gather",
    )(where, keep_count.T, keep_blocks, q_rows, keys_cache, values_cache)
    q_own = over_chips(q_copies)
    sib_packed = sibling(to_sib)
    partial = pl.pallas_call(
        attend_kernel,
        in_specs=[smem, smem, vmem, hbm, hbm, pl.BlockSpec(memory_space=pl.ANY)],
        out_specs=vmem,
        out_shape=jax.ShapeDtypeStruct((chips, PACK, HD), bf16),
        scratch_shapes=[pltpu.VMEM(tile, bf16)] * 2 + [dma((groups,))] * 2,
        compiler_params=pltpu.CompilerParams(vmem_limit_bytes=50 * MIB),
        name="attend",
    )(where, codes, q_own, keys_cache, values_cache, sib_packed)

    w_out_s, w_gate_s, w_up_s, w_down_s = w_out, w_gate, w_up, w_down
    res_s, gain_s = parity(residual_in, 1 - core), norm_gain
    w_out_sib = sibling(w_out_s)
    w_gate_sib = sibling(w_gate_s)
    w_up_sib = sibling(w_up_s)
    w_down_sib = sibling(w_down_s)
    extra = sibling(jnp.concatenate([res_s, jnp.broadcast_to(gain_s[None], (16, width))], axis=0))
    res = in_order(parity(residual_in, core), extra[:tokens])
    gain = in_order(jnp.broadcast_to(norm_gain[None], (16, width)), extra[tokens:])

    got = over_chips(partial)
    pad = ((0, 16 - STEPS), (0, 0))
    attended = pl.pallas_call(
        combine_kernel,
        in_specs=[vmem] * 4,
        out_specs=vmem,
        out_shape=jax.ShapeDtypeStruct((ROWS, HD), bf16),
        compiler_params=params,
        name="combine",
    )(
        got,
        q_rows,
        jnp.pad(new_keys.reshape(STEPS, KV * HD), pad),
        jnp.pad(new_values.reshape(STEPS, KV * HD), pad),
    )

    all_attended = over_chips(jnp.broadcast_to(attended[None], (chips, ROWS, HD)))
    projected = pl.pallas_call(
        project_kernel,
        in_specs=[smem, vmem, vmem, vmem],
        out_specs=vmem,
        out_shape=jax.ShapeDtypeStruct((tokens, 2 * width), bf16),
        scratch_shapes=[pltpu.VMEM((chips * ROWS, HD), f32)],
        compiler_params=params,
        name="project",
    )(where, all_attended, w_out, w_out_sib)
    parts = heads(projected)

    shares, stream, w_down_own, w_down_sib = pl.pallas_call(
        gate_up_kernel,
        in_specs=[smem] + [vmem] * 6 + [hbm] * 6,
        out_specs=[vmem] * 4,
        out_shape=[
            jax.ShapeDtypeStruct((chips, 4 * tokens + 16, HD), bf16),
            jax.ShapeDtypeStruct((tokens, 2 * width), f32),
            jax.ShapeDtypeStruct(w_down.shape, bf16),
            jax.ShapeDtypeStruct(w_down.shape, bf16),
        ],
        scratch_shapes=[pltpu.VMEM(w_gate.shape, bf16)] * 4 + [dma((4, 8)), dma((2,))],
        compiler_params=params,
        name="gate_up",
    )(where, *parts, res, gain, w_gate, w_up, w_gate_sib, w_up_sib, w_down, w_down_sib)

    got_shares = over_chips(shares)
    down = pl.pallas_call(
        down_kernel,
        in_specs=[smem, vmem, vmem, vmem],
        out_specs=vmem,
        out_shape=jax.ShapeDtypeStruct((chips, tokens, 2 * width), bf16),
        compiler_params=params,
        name="down",
    )(where, got_shares, w_down_own, w_down_sib)

    lowered = jnp.sum(over_chips(down).astype(f32), axis=0)
    rounded = lax.reduce_precision(lowered, 8, 7).astype(bf16)
    l0, l1, l2, l3 = (each.astype(f32) for each in heads(rounded))
    final = (stream + ((l0 + l1) + (l2 + l3))).astype(bf16)
    low, high = final[:, :width], final[:, width:]
    keep = jnp.where(core == 0, low, high)
    come = sibling(jnp.where(core == 0, high, low))
    even = jnp.where(core == 0, keep, come).reshape(STEPS, chips, 1, width)
    odd = jnp.where(core == 0, come, keep).reshape(STEPS, chips, 1, width)
    layer_out = jnp.concatenate([even, odd], axis=2).reshape(STEPS, holders, width)
    return (attended.reshape(STEPS, 1, HQ * HD), layer_out)


def solution(mesh):
    placed = (
        P(None, "seq", "head"),
        P(None, "seq", "head"),
        P(None, "head", None),
        P(None, "head"),
        P(None, "seq", "head"),
        P(None, "seq", "head"),
        P(None, "seq", "head"),
        P(None, None, "seq"),
        P("seq"),
        P("head", "seq"),
        P("seq", "head"),
        P("seq", "head"),
        P(("head", "seq"), None),
    )
    return jax.shard_map(
        on_device,
        mesh=mesh,
        in_specs=placed,
        out_specs=(P(None, "seq", "head"), P(None, None, "seq")),
        check_vma=False,
    )
```

```python
import functools

import jax
import jax.numpy as jnp
from jax import lax
from jax.experimental import pallas as pl
from jax.experimental.pallas import tpu as pltpu
from jax.sharding import PartitionSpec as P

D = 8192
H = 64
KVH = 8
HD = 128
BLK = 64
CAP = 4
GROUPS = H // KVH

masked_score = -1e30
norm_eps = 1e-06
score_scale = HD ** (-0.5)

f32 = jnp.float32
bf16 = jnp.bfloat16
MIB = 1 << 20

STEPS = 3
KV = 2
HQ = KV * GROUPS
ROWS = STEPS * HQ
PACK = ROWS + 16


def dot(a, b, ca=1, cb=0):
    return lax.dot_general(a, b, (((ca,), (cb,)), ((), ())), preferred_element_type=f32)


def first_head_rows():
    rows = lax.broadcasted_iota(jnp.int32, (ROWS, 1), 0)
    return (rows // GROUPS) % KV == 0


def two_head_queries(q, first):
    zero = jnp.zeros_like(q)
    return jnp.concatenate([jnp.where(first, q, zero), jnp.where(first, zero, q)], axis=1)


def per_head(values, first):
    return jnp.where(first, values[:, :HD], values[:, HD:])


def pack_prompt(prompt, codes, k_ref, v_ref, packed_ref, sem):
    half = CAP * BLK
    for h in range(KV):
        lanes = pl.ds(h * HD, HD)
        for s in range(CAP):
            at = pl.multiple_of(((codes[h] >> (3 * s)) & 7) * BLK, BLK)
            for part, cache_ref in enumerate((k_ref, v_ref)):
                pltpu.make_async_copy(
                    cache_ref.at[prompt, pl.ds(at, BLK), lanes],
                    packed_ref.at[pl.ds(part * half + s * BLK, BLK), lanes],
                    sem,
                ).start()


def gather_kernel(
    where_ref, count_ref, lists_ref, q_ref, k_ref, v_ref, out_ref, q_out, codes_ref,
    wide_ref, scalar_ref, packed_ref, list_sem, q_sems, in_sems, out_sems,
):
    spread = [
        pltpu.make_async_copy(q_ref, q_out.at[i], q_sems.at[i]) for i in range(q_out.shape[0])
    ]
    for copy in spread:
        copy.start()
    core = where_ref[1]
    per_dev = k_ref.shape[1] // BLK
    base = where_ref[0] * per_dev
    sib_base = (where_ref[0] + 1 - 2 * core) * per_dev
    lists = lists_ref[...]
    lane = lax.broadcasted_iota(jnp.int32, lists.shape, 2)
    valid = (lists > 0) | (lane == 0)
    before = jnp.sum(jnp.where(valid & (lists < base), 1.0, 0.0), axis=2, keepdims=True)
    local = lists - base
    mine = valid & (local >= 0) & (local < per_dev)
    theirs = valid & (lists >= sib_base) & (lists < sib_base + per_dev)
    rank = jnp.clip(lane - before.astype(jnp.int32), 0, CAP - 1)
    share = jnp.where(mine, jnp.left_shift(local, 3 * rank) + (1 << 12), 0)
    share = share + jnp.where(theirs, 1 << 15, 0)
    code = jnp.sum(share.astype(f32), axis=2, keepdims=True).astype(jnp.int32)
    spot = lax.broadcasted_iota(jnp.int32, lists.shape, 0) * KV + lax.broadcasted_iota(
        jnp.int32, lists.shape, 1
    )
    wide_ref[...] = jnp.sum(jnp.sum(jnp.where(lane == spot, code, 0), axis=0), axis=0, keepdims=True)
    listed = pltpu.make_async_copy(wide_ref, scalar_ref, list_sem)
    listed.start()
    listed.wait()

    def code_of(prompt, h):
        return jnp.where(count_ref[h, prompt] > 0, scalar_ref[0, prompt * KV + h], 0)

    chips = packed_ref.shape[0]
    groups = in_sems.shape[0]
    size = chips // groups
    for g in range(groups):

        def one(i, carry):
            chip = g * size + i
            prompt = chip * 2 + 1 - core
            codes = [code_of(prompt, h) for h in range(KV)]
            pack_prompt(prompt, codes, k_ref, v_ref, packed_ref.at[chip], in_sems.at[g])
            for h in range(KV):
                codes_ref[chip * KV + h] = code_of(chip * 2 + core, h)
            return carry

        lax.fori_loop(0, size, one, 0)
    leaving = []
    for g in range(groups):
        at = pl.ds(g * size, size)
        pltpu.make_async_copy(packed_ref.at[at], packed_ref.at[at], in_sems.at[g]).wait()
        leaving.append(pltpu.make_async_copy(packed_ref.at[at], out_ref.at[at], out_sems.at[g]))
        leaving[-1].start()
    for copy in leaving + spread:
        copy.wait()


def attend_kernel(
    where_ref, codes_ref, q_ref, k_ref, v_ref, sib_hbm, out_ref, own_ref, sib_ref, own_sems, sib_sems
):
    core = where_ref[1]
    half = CAP * BLK
    chips = q_ref.shape[0]
    groups = own_sems.shape[0]
    size = chips // groups
    first = first_head_rows()
    lane = lax.broadcasted_iota(jnp.int32, (ROWS, HD), 1)
    slot_lane = lax.broadcasted_iota(jnp.int32, (ROWS, half), 1)
    unit = (
        lax.broadcasted_iota(jnp.int32, (16, HD), 0) == lax.broadcasted_iota(jnp.int32, (16, HD), 1)
    ).astype(bf16)

    def from_sib(g):
        at = pl.ds(g * size, size)
        return pltpu.make_async_copy(sib_hbm.at[at], sib_ref.at[at], sib_sems.at[g])

    def fetch(g):
        from_sib(g).start()

        def one(i, carry):
            chip = g * size + i
            codes = [codes_ref[chip * KV + h] for h in range(KV)]
            pack_prompt(chip * 2 + core, codes, k_ref, v_ref, own_ref.at[chip], own_sems.at[g])
            return carry

        lax.fori_loop(0, size, one, 0)

    def score_of(chip):
        queries = two_head_queries(q_ref[chip], first)
        scores, keeps = [], []
        for shift, blocks_ref in ((12, own_ref), (15, sib_ref)):
            ends = [((codes_ref[chip * KV + h] >> shift) & 7) * BLK for h in range(KV)]
            keeps.append(slot_lane < jnp.where(first, ends[0], ends[1]))
            scores.append(dot(queries, blocks_ref[chip, :half, :], 1, 1))
        return jnp.concatenate(keeps, axis=1), jnp.concatenate(scores, axis=1)

    def weigh(keep, score):
        score = jnp.where(keep, score * score_scale, masked_score)
        top = jnp.max(score, axis=1, keepdims=True).astype(bf16).astype(f32)
        weight = jnp.where(keep, jnp.exp(score - top), 0.0).astype(bf16)
        return top, weight, jnp.sum(weight.astype(f32), axis=1, keepdims=True)

    def store(chip, top, weight, total):
        summed = per_head(
            dot(weight[:, :half], own_ref[chip, half:, :])
            + dot(weight[:, half:], sib_ref[chip, half:, :]),
            first,
        )
        total_hi = total.astype(bf16).astype(f32)
        notes = jnp.where(
            lane == 0, top, jnp.where(lane == 1, total_hi, jnp.where(lane == 2, total - total_hi, 0.0))
        ).astype(bf16)
        notes = jnp.concatenate([notes, jnp.zeros((HD - ROWS, HD), bf16)], axis=0)
        out_ref[chip, :ROWS, :] = summed.astype(bf16)
        out_ref[chip, ROWS:, :] = dot(unit, notes, 1, 1).astype(bf16)

    for g in range(groups):
        fetch(g)
    for g in range(groups):
        at = pl.ds(g * size, size)
        pltpu.make_async_copy(own_ref.at[at], own_ref.at[at], own_sems.at[g]).wait()
        from_sib(g).wait()
        chips_now = range(g * size, (g + 1) * size)
        scored = [score_of(chip) for chip in chips_now]
        weighed = [weigh(*each) for each in scored]
        for chip, each in zip(chips_now, weighed):
            store(chip, *each)


def combine_kernel(got_ref, q_ref, nk_ref, nv_ref, out_ref):
    holders = got_ref.shape[0]
    notes = got_ref[:, ROWS:, :].reshape(holders * 16, HD)
    row = lax.broadcasted_iota(jnp.int32, (holders * 16, HD), 0)
    col = lax.broadcasted_iota(jnp.int32, (holders * 16, HD), 1)
    pick = ((col == (row % 16) * holders + row // 16) & (row % 16 < 3)).astype(bf16)
    columns = dot(notes, pick, 0, 0)[:ROWS]
    tops = columns[:, :holders]
    totals = columns[:, holders : 2 * holders] + columns[:, 2 * holders : 3 * holders]
    first = first_head_rows()
    new_score = dot(two_head_queries(q_ref[...], first), nk_ref[...], 1, 1) * score_scale
    step = lax.broadcasted_iota(jnp.int32, new_score.shape, 0) // HQ
    token = lax.broadcasted_iota(jnp.int32, new_score.shape, 1)
    causal = token <= step
    new_score = jnp.where(causal, new_score, masked_score)
    top = jnp.maximum(
        jnp.max(tops, axis=1, keepdims=True), jnp.max(new_score, axis=1, keepdims=True)
    )
    share = jnp.exp(tops - top)
    new_weight = jnp.where(causal, jnp.exp(new_score - top), 0.0).astype(bf16)
    total = jnp.sum(share * totals, axis=1, keepdims=True) + jnp.sum(
        new_weight.astype(f32), axis=1, keepdims=True
    )
    summed = per_head(dot(new_weight, nv_ref[...]), first)
    for i in range(holders):
        summed = summed + share[:, i : i + 1] * got_ref[i, :ROWS, :].astype(f32)
    out_ref[...] = (summed / total).astype(bf16)


def project_kernel(where_ref, got_ref, own_ref, sib_ref, out_ref, wide_ref):
    core = where_ref[1]
    chips = got_ref.shape[0]
    wide_ref[...] = got_ref[...].reshape(chips * ROWS, HD).astype(f32)
    own = jnp.zeros((STEPS * chips, own_ref.shape[1]), f32)
    sib = jnp.zeros((STEPS * chips, own_ref.shape[1]), f32)
    for pair in range(HQ // 2):
        parts = []
        for h in (2 * pair, 2 * pair + 1):
            parts.append(
                jnp.concatenate(
                    [wide_ref[pl.ds(t * HQ + h, chips, stride=ROWS), :] for t in range(STEPS)], axis=0
                )
            )
        rows = jnp.concatenate(parts, axis=1).astype(bf16)
        at = slice(pair * 2 * HD, (pair + 1) * 2 * HD)
        own = own + dot(rows, own_ref[at, :])
        sib = sib + dot(rows, sib_ref[at, :])
    half = own_ref.shape[1]
    out_ref[:, :half] = jnp.where(core == 0, own, sib).astype(bf16)
    out_ref[:, half:] = jnp.where(core == 0, sib, own).astype(bf16)


def gate_up_kernel(
    where_ref, p0, p1, p2, p3, res_ref, gain_ref, g_own_hbm, u_own_hbm, g_sib_hbm, u_sib_hbm,
    d_own_hbm, d_sib_hbm, out_ref, stream_ref, d_own_ref, d_sib_ref, g_own, u_own, g_sib, u_sib,
    part_sems, whole_sems,
):
    core = where_ref[1]
    parts = part_sems.shape[1]
    columns = g_own.shape[1] // parts
    brought = []
    for part in range(parts):
        at = (slice(None), pl.ds(part * columns, columns))
        brought.append(
            [
                pltpu.make_async_copy(source.at[at], target.at[at], part_sems.at[n, part])
                for n, (source, target) in enumerate(
                    (
                        (g_own_hbm, g_own),
                        (g_sib_hbm, g_sib),
                        (u_own_hbm, u_own),
                        (u_sib_hbm, u_sib),
                    )
                )
            ]
        )
        for copy in brought[-1]:
            copy.start()
    later = [
        pltpu.make_async_copy(source, target, whole_sems.at[n])
        for n, (source, target) in enumerate(((d_own_hbm, d_own_ref), (d_sib_hbm, d_sib_ref)))
    ]
    for copy in later:
        copy.start()
    half = g_own.shape[0]
    chips = out_ref.shape[0]
    stream = res_ref[...].astype(f32) + (
        (p0[...].astype(f32) + p1[...].astype(f32)) + (p2[...].astype(f32) + p3[...].astype(f32))
    )
    stream_ref[...] = stream
    scaled = stream * gain_ref[0:1, :].astype(f32)
    mine = jnp.where(core == 0, scaled[:, :half], scaled[:, half:]).astype(bf16)
    other = jnp.where(core == 0, scaled[:, half:], scaled[:, :half]).astype(bf16)
    square = jnp.sum(stream * stream, axis=1, keepdims=True)
    square_hi = square.astype(bf16).astype(f32)
    tokens = square.shape[0]
    lane = lax.broadcasted_iota(jnp.int32, (tokens, HD), 1)
    notes = jnp.where(
        lane == 0, square_hi, jnp.where(lane == 1, square - square_hi, 0.0)
    ).astype(bf16)
    notes = jnp.concatenate([notes, jnp.zeros((HD - tokens, HD), bf16)], axis=0)
    unit = (
        lax.broadcasted_iota(jnp.int32, (16, HD), 0) == lax.broadcasted_iota(jnp.int32, (16, HD), 1)
    ).astype(bf16)
    squares = dot(unit, notes, 1, 1).astype(bf16)
    wide = g_own.shape[1] // chips

    def store(k, gate, up):
        for part in range(2):
            at = slice(part * HD, (part + 1) * HD)
            out_ref[k, part * tokens : (part + 1) * tokens, :] = gate[:, at]
            out_ref[k, (2 + part) * tokens : (3 + part) * tokens, :] = up[:, at]
        out_ref[k, 4 * tokens :, :] = squares

    ready = None
    for k in range(chips):
        if k % (chips // parts) == 0:
            for copy in brought[k // (chips // parts)]:
                copy.wait()
        at = slice(k * wide, (k + 1) * wide)
        gate = dot(mine, g_own[:, at]) + dot(other, g_sib[:, at])
        up = dot(mine, u_own[:, at]) + dot(other, u_sib[:, at])
        if ready:
            store(*ready)
        ready = k, gate.astype(bf16), up.astype(bf16)
    store(*ready)
    for copy in later:
        copy.wait()


def down_kernel(where_ref, got_ref, own_ref, sib_ref, out_ref):
    core = where_ref[1]
    chips, tokens, width = out_ref.shape
    total = got_ref[0].astype(f32)
    for i in range(1, chips):
        total = total + got_ref[i].astype(f32)
    square = total[4 * tokens : 4 * tokens + 1, :] + total[4 * tokens + 1 : 4 * tokens + 2, :]
    scale_row = lax.rsqrt(square / D + norm_eps)
    row = lax.broadcasted_iota(jnp.int32, (tokens, HD), 0)
    col = lax.broadcasted_iota(jnp.int32, (tokens, HD), 1)
    scale = jnp.sum(jnp.where(row == col, scale_row, 0.0), axis=1, keepdims=True)
    halves = []
    for part in range(2):
        gate = total[part * tokens : (part + 1) * tokens] * scale
        up = total[(2 + part) * tokens : (3 + part) * tokens] * scale
        halves.append(gate / (1.0 + jnp.exp(-gate)) * up)
    mine = jnp.where(core == 0, halves[0], halves[1]).astype(bf16)
    other = jnp.where(core == 0, halves[1], halves[0]).astype(bf16)
    rows = jnp.concatenate([mine, other], axis=1)
    for k in range(chips):
        at = slice(k * width, (k + 1) * width)
        out_ref[k] = dot(rows, jnp.concatenate([own_ref[:, at], sib_ref[:, at]], axis=0)).astype(bf16)


def on_device(
    keys_cache,
    values_cache,
    keep_blocks,
    keep_count,
    queries,
    new_keys,
    new_values,
    residual_in,
    norm_gain,
    w_out,
    w_gate,
    w_up,
    w_down,
):
    holders = lax.axis_size("seq")
    chips = holders // 2
    holder = lax.axis_index("seq").astype(jnp.int32)
    core = holder % 2
    prompts, positions = keys_cache.shape[:2]
    per_dev = positions // BLK
    list_length = keep_blocks.shape[2]
    tokens = STEPS * chips
    width = residual_in.shape[2]
    where = jnp.stack([holder, core])
    smem = pl.BlockSpec(memory_space=pltpu.SMEM)
    vmem = pl.BlockSpec(memory_space=pltpu.VMEM)
    hbm = pl.BlockSpec(memory_space=pltpu.HBM)
    params = pltpu.CompilerParams(vmem_limit_bytes=24 * MIB)

    same_core = [[2 * i + c for i in range(chips)] for c in range(2)]
    swap = [(i, i ^ 1) for i in range(holders)]

    def over_chips(x):
        return lax.all_to_all(
            x, "seq", split_axis=0, concat_axis=0, tiled=True, axis_index_groups=same_core
        )

    def sibling(x):
        return lax.ppermute(x, "seq", swap)

    def heads(x):
        return [x] + [lax.ppermute(x, "head", [(i, i ^ s) for i in range(4)]) for s in (1, 2, 3)]

    def parity(x, which):
        x = x.reshape(STEPS, chips, 2, width)
        return lax.dynamic_slice_in_dim(x, which, 1, 2).reshape(tokens, width)

    def in_order(own, sib):
        low = jnp.where(core == 0, own, sib)
        high = jnp.where(core == 0, sib, own)
        return jnp.concatenate([low, high], axis=1)

    q_rows = queries.reshape(ROWS, HD)

    half = CAP * BLK
    tile = (chips, 2 * half, KV * HD)
    groups = 4
    dma = pltpu.SemaphoreType.DMA
    to_sib, q_copies, codes = pl.pallas_call(
        gather_kernel,
        in_specs=[smem, smem, vmem, vmem, hbm, hbm],
        out_specs=[hbm, hbm, smem],
        out_shape=[
            jax.ShapeDtypeStruct(tile, bf16),
            jax.ShapeDtypeStruct((chips, ROWS, HD), bf16),
            jax.ShapeDtypeStruct((chips * KV,), jnp.int32),
        ],
        scratch_shapes=[
            pltpu.VMEM((1, list_length), jnp.int32),
            pltpu.SMEM((1, list_length), jnp.int32),
            pltpu.VMEM(tile, bf16),
            dma,
            dma((chips,)),
            dma((2 * groups,)),
            dma((2 * groups,)),
        ],
        compiler_params=pltpu.CompilerParams(vmem_limit_bytes=50 * MIB),
        name="gather",
    )(where, keep_count.T, keep_blocks, q_rows, keys_cache, values_cache)
    q_own = over_chips(q_copies)
    sib_packed = sibling(to_sib)
    partial = pl.pallas_call(
        attend_kernel,
        in_specs=[smem, smem, vmem, hbm, hbm, pl.BlockSpec(memory_space=pl.ANY)],
        out_specs=vmem,
        out_shape=jax.ShapeDtypeStruct((chips, PACK, HD), bf16),
        scratch_shapes=[pltpu.VMEM(tile, bf16)] * 2 + [dma((groups,))] * 2,
        compiler_params=pltpu.CompilerParams(vmem_limit_bytes=50 * MIB),
        name="attend",
    )(where, codes, q_own, keys_cache, values_cache, sib_packed)

    w_out_s, w_gate_s, w_up_s, w_down_s = w_out, w_gate, w_up, w_down
    res_s, gain_s = parity(residual_in, 1 - core), norm_gain
    w_out_sib = sibling(w_out_s)
    w_gate_sib = sibling(w_gate_s)
    w_up_sib = sibling(w_up_s)
    w_down_sib = sibling(w_down_s)
    extra = sibling(jnp.concatenate([res_s, jnp.broadcast_to(gain_s[None], (16, width))], axis=0))
    res = in_order(parity(residual_in, core), extra[:tokens])
    gain = in_order(jnp.broadcast_to(norm_gain[None], (16, width)), extra[tokens:])

    got = over_chips(partial)
    pad = ((0, 16 - STEPS), (0, 0))
    attended = pl.pallas_call(
        combine_kernel,
        in_specs=[vmem] * 4,
        out_specs=vmem,
        out_shape=jax.ShapeDtypeStruct((ROWS, HD), bf16),
        compiler_params=params,
        name="combine",
    )(
        got,
        q_rows,
        jnp.pad(new_keys.reshape(STEPS, KV * HD), pad),
        jnp.pad(new_values.reshape(STEPS, KV * HD), pad),
    )

    all_attended = over_chips(jnp.broadcast_to(attended[None], (chips, ROWS, HD)))
    projected = pl.pallas_call(
        project_kernel,
        in_specs=[smem, vmem, vmem, vmem],
        out_specs=vmem,
        out_shape=jax.ShapeDtypeStruct((tokens, 2 * width), bf16),
        scratch_shapes=[pltpu.VMEM((chips * ROWS, HD), f32)],
        compiler_params=params,
        name="project",
    )(where, all_attended, w_out, w_out_sib)
    parts = heads(projected)

    shares, stream, w_down_own, w_down_sib = pl.pallas_call(
        gate_up_kernel,
        in_specs=[smem] + [vmem] * 6 + [hbm] * 6,
        out_specs=[vmem] * 4,
        out_shape=[
            jax.ShapeDtypeStruct((chips, 4 * tokens + 16, HD), bf16),
            jax.ShapeDtypeStruct((tokens, 2 * width), f32),
            jax.ShapeDtypeStruct(w_down.shape, bf16),
            jax.ShapeDtypeStruct(w_down.shape, bf16),
        ],
        scratch_shapes=[pltpu.VMEM(w_gate.shape, bf16)] * 4 + [dma((4, 8)), dma((2,))],
        compiler_params=params,
        name="gate_up",
    )(where, *parts, res, gain, w_gate, w_up, w_gate_sib, w_up_sib, w_down, w_down_sib)

    got_shares = over_chips(shares)
    down = pl.pallas_call(
        down_kernel,
        in_specs=[smem, vmem, vmem, vmem],
        out_specs=vmem,
        out_shape=jax.ShapeDtypeStruct((chips, tokens, 2 * width), bf16),
        compiler_params=params,
        name="down",
    )(where, got_shares, w_down_own, w_down_sib)

    lowered = jnp.sum(over_chips(down).astype(f32), axis=0)
    rounded = lax.reduce_precision(lowered, 8, 7).astype(bf16)
    l0, l1, l2, l3 = (each.astype(f32) for each in heads(rounded))
    final = (stream + ((l0 + l1) + (l2 + l3))).astype(bf16)
    low, high = final[:, :width], final[:, width:]
    keep = jnp.where(core == 0, low, high)
    come = sibling(jnp.where(core == 0, high, low))
    even = jnp.where(core == 0, keep, come).reshape(STEPS, chips, 1, width)
    odd = jnp.where(core == 0, come, keep).reshape(STEPS, chips, 1, width)
    layer_out = jnp.concatenate([even, odd], axis=2).reshape(STEPS, holders, width)
    return (attended.reshape(STEPS, 1, HQ * HD), layer_out)


def solution(mesh):
    placed = (
        P(None, "seq", "head"),
        P(None, "seq", "head"),
        P(None, "head", None),
        P(None, "head"),
        P(None, "seq", "head"),
        P(None, "seq", "head"),
        P(None, "seq", "head"),
        P(None, None, "seq"),
        P("seq"),
        P("head", "seq"),
        P("seq", "head"),
        P("seq", "head"),
        P(("head", "seq"), None),
    )
    return jax.shard_map(
        on_device,
        mesh=mesh,
        in_specs=placed,
        out_specs=(P(None, "seq", "head"), P(None, None, "seq")),
        check_vma=False,
    )
```
